128 devices in a mesh: slide: 4 (over y), tile: 32 (over z, x, core).
Axes of the slice: x: 4, y: 4, z: 4, core: 2. Of those that a mesh axis runs over, the one named last changes fastest.
Arguments:
- tiles: bfloat16 [128, 256, 1536], P('tile'), may hold values from -6 to 6
- w_in: bfloat16 [1536, 6144], P(None, 'slide'), may hold values from -0.15625 to 0.15625
- w_out: bfloat16 [6144, 1536], P('slide'), may hold values from -0.078125 to 0.078125
- w_proj: bfloat16 [1536, 768], replicated, may hold values from -0.15625 to 0.15625
- w_qkv: bfloat16 [768, 2304], replicated, may hold values from -0.25 to 0.25
- w_attn_out: bfloat16 [768, 768], replicated, may hold values from -0.21875 to 0.21875
- slide_of_tile: int32 [128], replicated, may hold values from 0 to 15, as said below
- order_of_tile: int32 [128], replicated, may hold values from 0 to 56, as said below
- slide_counts: int32 [16], replicated, may hold values from 1 to 57, as said below
- seg_len: int32 [3], replicated, may hold values from 2 to 16
- slide_cot: float32 [16, 768], P('slide'), may hold values from -6 to 6
Outputs:
- slide_embed: float32 [16, 768], P('slide')
- grad_in: float32 [1536, 6144], P('tile', 'slide')
- grad_out: float32 [6144, 1536], P(('slide', 'tile'))
The draws below stay inside these ranges and needn't reach their ends.
Inputs may be any that keep to these rules, and one draw needn't show every extreme that they name: Every slide has at least one tile; slide_counts sums to 128; exactly one slide has the most tiles. `slide_of_tile`: slide g is named by exactly slide_counts[g] tiles. `order_of_tile`: the tiles of slide g carry the positions 0 to slide_counts[g] - 1, each once.
All inputs are finite; a program needn't handle non-finite values.
Results may differ from the reference program's by a relative error of at most 0.02.
Values may be sent and summed in bfloat16 or wider, within the bound.
No kernel may reach another device: no remote copies, remote signals or barrier semaphores. Data moves between devices by JAX's collectives and lax.ppermute only.
A program may use at most 128 MiB of HBM per device.

```python
import math
import jax
import jax.numpy as jnp
from jax import lax

D = 1536
FF = 6144
SD = 768
SH = 16
P_SIZE = 256
BRANCHES = 3
TILE_DEV = 4
TILES = 128
SLIDES = 16


def slide_layout(key):
    spare_tiles = TILES - SLIDES
    heavy_extra = (spare_tiles + 1) // 2
    light_extra = spare_tiles - heavy_extra
    labels = jax.random.permutation(jax.random.fold_in(key, 102), SLIDES).astype(jnp.int32)
    pick_codes = jax.random.randint(jax.random.fold_in(key, 101), (light_extra,), 0, (SLIDES - 1) * (SLIDES - 1))
    squares = jnp.arange(1, SLIDES - 1, dtype=jnp.int32) ** 2
    slide_rank = 1 + jnp.sum((squares[None, :] <= pick_codes[:, None]).astype(jnp.int32), axis=1)
    chosen = labels[slide_rank]
    slide_range = jnp.arange(SLIDES, dtype=jnp.int32)
    counts = 1 + jnp.sum((chosen[:, None] == slide_range[None, :]).astype(jnp.int32), axis=0)
    counts = counts + heavy_extra * (slide_range == labels[0]).astype(jnp.int32)
    slide_ends = jnp.cumsum(counts)
    starts = slide_ends - counts
    position = jnp.arange(TILES, dtype=jnp.int32)
    sorted_slide = jnp.sum((slide_ends[None, :] <= position[:, None]).astype(jnp.int32), axis=1)
    sorted_order = position - starts[sorted_slide]
    shuffle = jax.random.permutation(jax.random.fold_in(key, 103), TILES)
    slide_of = jnp.zeros((TILES,), jnp.int32).at[shuffle].set(sorted_slide)
    order_of = jnp.zeros((TILES,), jnp.int32).at[shuffle].set(sorted_order)
    return (counts.astype(jnp.int32), slide_of, order_of)


def draw_tiles(key, part):
    key = jax.random.fold_in(key, 7)
    offset_key = jax.random.fold_in(key, 1)
    noise_key = jax.random.fold_in(key, 2)
    offset = jax.random.normal(offset_key, (TILES, 1, D), jnp.float32)
    noise = jax.random.normal(noise_key, (TILES, P_SIZE, D), jnp.float32)
    return jnp.clip(offset + noise, -6.0, 6.0).astype(jnp.bfloat16)


def draw_slide_counts(key, part):
    layout = slide_layout(key)
    return layout[0]


def draw_slide_of_tile(key, part):
    layout = slide_layout(key)
    return layout[1]


def draw_order_of_tile(key, part):
    layout = slide_layout(key)
    return layout[2]


def shard_levels(own_key, shape, cuts, low, largest):
    loudness, own = 1.0, jax.random.fold_in(own_key, 6)
    for dim, blocks in cuts:
        heights = jnp.exp(jax.random.uniform(jax.random.fold_in(own, dim), (blocks,), jnp.float32, low / len(cuts), largest / len(cuts)))
        loudness = loudness * jnp.repeat(heights, shape[dim] // blocks).reshape([-1 if axis == dim else 1 for axis in range(len(shape))])
    return loudness


def centred(key, extent, scale, reach, cuts=(), held_as=jnp.bfloat16):
    level = shard_levels(key, extent, cuts, -0.22, 0.18) if cuts else 1.0
    entries = jax.random.normal(key, extent, jnp.float32) * scale * level
    return jnp.minimum(jnp.maximum(entries, -reach), reach).astype(held_as)


def setup_inputs(seed: int = 0) -> dict:
    splits = jax.random.split(jax.random.key(seed), 12)
    tiles = draw_tiles(jax.random.fold_in(splits[11], 71), 0)
    w_in = centred(splits[1], (D, FF), D ** -0.5, 0.15625, ((1, 4),))
    w_out = centred(splits[2], (FF, D), FF ** -0.5, 0.078125, ((0, 4),))
    w_proj = centred(splits[3], (D, SD), D ** -0.5, 0.15625)
    w_qkv = centred(splits[4], (SD, 3 * SD), (16 * SD // 25) ** -0.5, 0.25)
    w_attn_out = centred(splits[5], (SD, SD), SD ** -0.5, 0.21875)
    slide_of_tile = draw_slide_of_tile(jax.random.fold_in(splits[11], 71), 0)
    order_of_tile = draw_order_of_tile(jax.random.fold_in(splits[11], 71), 0)
    slide_counts = draw_slide_counts(jax.random.fold_in(splits[11], 71), 0)
    seg_len = jax.random.randint(splits[9], (BRANCHES,), 2, 17).astype(jnp.int32)
    slide_cot = centred(splits[10], (SLIDES, SD), 1.0, 6.0, ((0, 4),), jnp.float32)
    return dict(tiles=tiles, w_in=w_in, w_out=w_out, w_proj=w_proj, w_qkv=w_qkv, w_attn_out=w_attn_out, slide_of_tile=slide_of_tile, order_of_tile=order_of_tile, slide_counts=slide_counts, seg_len=seg_len, slide_cot=slide_cot)


epsilon = 1e-06

def normalize(values):
    values = values.astype(jnp.float32)
    centre = lax.optimization_barrier(jnp.mean(values, axis=-1, keepdims=True))
    shifted = values - centre
    spread = lax.optimization_barrier(jnp.mean(shifted * shifted, axis=-1, keepdims=True))
    return (shifted * lax.rsqrt(spread + epsilon)).astype(jnp.bfloat16)

def gelu_pair(preact):
    normal_cdf = 0.5 * (1.0 + lax.erf(preact * 0.7071067811865476))
    normal_pdf = jnp.exp(-0.5 * preact * preact) * 0.3989422804014327
    return (preact * normal_cdf, normal_cdf + preact * normal_pdf)

def multiplicity(slide_query, order_query, slide_key, order_key, seg_len):
    same_slide = slide_query[:, None] == slide_key[None, :]
    counted = jnp.zeros(same_slide.shape, jnp.float32)
    for branch in range(seg_len.shape[0]):
        seg_width = seg_len[branch]
        dilation = 2 ** branch
        same_block = order_query[:, None] // seg_width == order_key[None, :] // seg_width
        same_phase = order_query[:, None] % dilation == order_key[None, :] % dilation
        counted = counted + (same_slide & same_block & same_phase).astype(jnp.float32)
    return counted

def attend(query_rows, key_rows, value_rows, weight, head_count):
    query_count = query_rows.shape[0]
    key_count = key_rows.shape[0]
    head_dim = query_rows.shape[1] // head_count
    query_heads = query_rows.reshape(query_count, head_count, head_dim)
    key_heads = key_rows.reshape(key_count, head_count, head_dim)
    value_heads = value_rows.reshape(key_count, head_count, head_dim)
    scores = jnp.einsum('qhd,khd->hqk', query_heads, key_heads, precision=lax.Precision.HIGHEST) / math.sqrt(head_dim)
    allowed = (weight > 0.0)[None]
    scores = jnp.where(allowed, scores, -1e+30)
    row_max = lax.optimization_barrier(jnp.max(scores, axis=-1, keepdims=True))
    numerator = weight[None] * jnp.exp(scores - row_max)
    denominator = lax.optimization_barrier(jnp.sum(numerator, axis=-1, keepdims=True))
    context = jnp.einsum('hqk,khd->qhd', numerator / denominator, value_heads, precision=lax.Precision.HIGHEST)
    return context.reshape(query_count, head_count * head_dim)

def reference(tiles, w_in, w_out, w_proj, w_qkv, w_attn_out, slide_of_tile, order_of_tile, slide_counts, seg_len, slide_cot):
    blocks = tiles.reshape(TILES // TILE_DEV, TILE_DEV, P_SIZE, D)

    def forward_block(tile_block):
        normed = normalize(tile_block.reshape(TILE_DEV * P_SIZE, D))
        preact = jnp.dot(normed, w_in, preferred_element_type=jnp.float32)
        hidden = gelu_pair(preact)[0].astype(jnp.bfloat16)
        return lax.optimization_barrier(jnp.mean(hidden.reshape(TILE_DEV, P_SIZE, FF), axis=1, dtype=jnp.float32))
    pooled = lax.map(forward_block, blocks).reshape(TILES, FF)
    token_mean = lax.optimization_barrier(jnp.mean(tiles, axis=1, dtype=jnp.float32))
    branch_term = jnp.dot(pooled, w_out, precision=lax.Precision.HIGHEST, preferred_element_type=jnp.float32)
    embedding = (token_mean + branch_term).astype(jnp.bfloat16)
    slide_rows = jnp.dot(embedding, w_proj, preferred_element_type=jnp.float32).astype(jnp.bfloat16)
    qkv = jnp.dot(slide_rows, w_qkv, preferred_element_type=jnp.float32).astype(jnp.bfloat16)
    qkv_wide = lax.optimization_barrier(qkv).astype(jnp.float32)
    rows_wide = lax.optimization_barrier(slide_rows).astype(jnp.float32)
    weight = multiplicity(slide_of_tile, order_of_tile, slide_of_tile, order_of_tile, seg_len)
    slide_ids = jnp.arange(SLIDES, dtype=jnp.int32)
    assign = (slide_of_tile[None, :] == slide_ids[:, None]).astype(jnp.float32) / slide_counts[:, None].astype(jnp.float32)
    out_wide = w_attn_out.astype(jnp.float32)

    def slide_fn(query_rows, key_rows, value_rows, base_rows):
        context = attend(query_rows, key_rows, value_rows, weight, SH)
        attended = base_rows + jnp.dot(context, out_wide, precision=lax.Precision.HIGHEST)
        return jnp.dot(assign, attended, precision=lax.Precision.HIGHEST)
    slide_embed, pullback = jax.vjp(slide_fn, qkv_wide[:, :SD], qkv_wide[:, SD:2 * SD], qkv_wide[:, 2 * SD:], rows_wide)
    d_query, d_keys, d_values, d_direct = pullback(slide_cot)
    d_qkv = jnp.concatenate([d_query, d_keys, d_values], axis=1)
    d_slide = d_direct + jnp.dot(d_qkv, w_qkv.astype(jnp.float32).T, precision=lax.Precision.HIGHEST)
    d_embed = jnp.dot(d_slide, w_proj.astype(jnp.float32).T, precision=lax.Precision.HIGHEST)
    grad_out = jnp.dot(pooled.T, d_embed, precision=lax.Precision.HIGHEST)
    d_pooled = jnp.dot(d_embed, w_out.astype(jnp.float32).T, precision=lax.Precision.HIGHEST)
    pooled_blocks = d_pooled.reshape(TILES // TILE_DEV, TILE_DEV, FF)

    def backward_block(running, pieces):
        tile_block, d_block = pieces
        normed = normalize(tile_block.reshape(TILE_DEV * P_SIZE, D))
        preact = jnp.dot(normed, w_in, preferred_element_type=jnp.float32)
        gelu_slope = gelu_pair(preact)[1]
        d_preact = (gelu_slope.reshape(TILE_DEV, P_SIZE, FF) * (d_block / P_SIZE)[:, None, :]).reshape(TILE_DEV * P_SIZE, FF).astype(jnp.bfloat16)
        term = lax.dot_general(normed, d_preact, (((0,), (0,)), ((), ())), preferred_element_type=jnp.float32)
        return (running + term, None)
    grad_in, _ = lax.scan(backward_block, jnp.zeros((D, FF), jnp.float32), (blocks, pooled_blocks))
    return (slide_embed, grad_in, grad_out)
```

```python
import math

import jax
import jax.numpy as jnp
from jax import lax
from jax.experimental import pallas as pl
from jax.experimental.pallas import tpu as pltpu
from jax.sharding import PartitionSpec as P

HEADS = 16
EPSILON = 1e-06
MIB = 1 << 20
BF = jnp.bfloat16
F4 = jnp.float32


def dot_nn(a, b):
    return lax.dot_general(a, b, (((1,), (0,)), ((), ())), preferred_element_type=F4)


def dot_nt(a, b):
    return lax.dot_general(a, b, (((1,), (1,)), ((), ())), preferred_element_type=F4)


def dot_tn(a, b):
    return lax.dot_general(a, b, (((0,), (0,)), ((), ())), preferred_element_type=F4)


def halves(value):
    high = value.astype(BF)
    return high, (value - high.astype(F4)).astype(BF)


def standardise(values):
    width = values.shape[1]
    centre = jnp.sum(values, axis=1, keepdims=True) * (1.0 / width)
    shifted = values - centre
    spread = jnp.sum(shifted * shifted, axis=1, keepdims=True) * (1.0 / width)
    return shifted * lax.rsqrt(spread + EPSILON)


def gelu_pair(a):
    bell = jnp.exp(a * a * -0.5)
    t = 1.0 / (1.0 + jnp.abs(a) * (0.3275911 * 0.7071067811865476))
    series = t * (0.127414796 + t * (-0.142248368 + t * (0.7107068705 + t * (-0.7265760135 + t * 0.5307027145))))
    tail = series * bell
    phi = jnp.where(a < 0.0, tail, 1.0 - tail)
    return a * phi, phi + a * (bell * 0.3989422804014327)


def forward_kernel(tiles, w_in, w_out, cot, slope, pooled, shared, token_mean, normed, total):
    step = pl.program_id(0)
    tile_count = token_mean.shape[0]
    patches = tiles.shape[0] // tile_count

    @pl.when(step == 0)
    def _():
        for tile in range(tile_count):
            rows = pl.ds(tile * patches, patches)
            values = tiles[rows, :].astype(F4)
            token_mean[pl.ds(tile, 1), :] = jnp.sum(values, axis=0, keepdims=True) * (1.0 / patches)
            normed[rows, :] = standardise(values).astype(BF)
        total[...] = jnp.zeros_like(total)

    means = []
    for tile in range(tile_count):
        rows = pl.ds(tile * patches, patches)
        value, rate = gelu_pair(dot_nn(normed[rows, :], w_in[...]))
        slope[rows, :] = rate.astype(BF)
        means.append(jnp.sum(value, axis=0, keepdims=True) * (1.0 / patches))
    high, low = halves(jnp.concatenate(means, axis=0))
    both = jnp.concatenate([high, low], axis=0)
    pooled[...] = both
    total[...] += dot_nn(both, w_out[...])

    @pl.when(step == pl.num_programs(0) - 1)
    def _():
        width = total.shape[1]
        shared[:, :width] = total[:tile_count, :] + total[tile_count:, :]
        shared[:, width:] = cot[...]


def forward(tiles, w_in, w_out, cot, tile_count):
    tokens, width = tiles.shape
    hidden = w_in.shape[1]
    block = 256
    slide_width = cot.shape[1]
    return pl.pallas_call(
        forward_kernel,
        grid=(hidden // block,),
        in_specs=[
            pl.BlockSpec((tokens, width), lambda j: (0, 0)),
            pl.BlockSpec((width, block), lambda j: (0, j)),
            pl.BlockSpec((block, width), lambda j: (j, 0)),
            pl.BlockSpec((tile_count, slide_width), lambda j: (0, 0)),
        ],
        out_specs=[
            pl.BlockSpec((tokens, block), lambda j: (0, j)),
            pl.BlockSpec((2 * tile_count, block), lambda j: (0, j)),
            pl.BlockSpec((tile_count, width + slide_width), lambda j: (0, 0)),
            pl.BlockSpec((tile_count, width), lambda j: (0, 0)),
        ],
        out_shape=[
            jax.ShapeDtypeStruct((tokens, hidden), BF),
            jax.ShapeDtypeStruct((2 * tile_count, hidden), BF),
            jax.ShapeDtypeStruct((tile_count, width + slide_width), F4),
            jax.ShapeDtypeStruct((tile_count, width), F4),
        ],
        scratch_shapes=[pltpu.VMEM((tokens, width), BF), pltpu.VMEM((2 * tile_count, width), F4)],
        compiler_params=pltpu.CompilerParams(vmem_limit_bytes=40 * MIB),
        name="forward",
    )(tiles, w_in, w_out, cot)


def transpose_kernel(place_a, place_b, tiles, out_a, out_b):
    normed_t = standardise(tiles[...].astype(F4)).astype(BF).T
    rows = out_a.shape[0] // place_a.shape[0]
    for block in range(place_a.shape[0]):
        piece = normed_t[block * rows : (block + 1) * rows, :]
        out_a[pl.ds(pl.multiple_of(place_a[block] * rows, 16), rows), :] = piece
        out_b[pl.ds(pl.multiple_of(place_b[block] * rows, 16), rows), :] = piece


def transposed(tiles, place_a, place_b, patches):
    tokens, width = tiles.shape
    spec = pl.BlockSpec((width, patches), lambda i: (0, i))
    return pl.pallas_call(
        transpose_kernel,
        grid=(tokens // patches,),
        in_specs=[
            pl.BlockSpec(memory_space=pltpu.SMEM),
            pl.BlockSpec(memory_space=pltpu.SMEM),
            pl.BlockSpec((patches, width), lambda i: (i, 0)),
        ],
        out_specs=[spec, spec],
        out_shape=[jax.ShapeDtypeStruct((width, tokens), BF)] * 2,
        compiler_params=pltpu.CompilerParams(vmem_limit_bytes=24 * MIB),
        cost_estimate=pl.CostEstimate(flops=20_000_000, bytes_accessed=9_000_000, transcendentals=0),
        name="transposed",
    )(place_a, place_b, tiles)


def embed_kernel(place, own, one, two, three, token_mean, counts, pooled, out, cot_all):
    width = token_mean.shape[1]
    half = width // 2
    total = (own[:, :width] + two[:, :width]) + (one[:, :width] + three[:, :width])
    embedding = total + token_mean[...]
    eight = jnp.concatenate([embedding[:, :half], embedding[:, half:]], axis=0)
    out[:, :half] = jnp.concatenate([eight] * (out.shape[0] // 8), axis=0).astype(BF)
    out[:, half:] = pooled[...]
    parts = [own[:, width:], one[:, width:], two[:, width:], three[:, width:]]
    blocks = []
    for group in range(4):
        back = jnp.bitwise_and(place[0] - group, 3)
        block = parts[0]
        for shift in range(1, 4):
            block = jnp.where(back == shift, parts[shift], block)
        blocks.append(block)
    cot_all[...] = jnp.concatenate(blocks, axis=0) / counts[...].astype(F4)


def embed(place, parts, token_mean, counts, pooled, peers):
    tile_count, width = token_mean.shape
    slide_width = parts[0].shape[1] - width
    return pl.pallas_call(
        embed_kernel,
        in_specs=[pl.BlockSpec(memory_space=pltpu.SMEM)] + [pl.BlockSpec(memory_space=pltpu.VMEM)] * 7,
        out_shape=[
            jax.ShapeDtypeStruct((peers * 8, width // 2 + 128), BF),
            jax.ShapeDtypeStruct((16, slide_width), F4),
        ],
        name="embed",
    )(place, *parts, token_mean, counts, pooled)


def attention_kernel(
    place,
    seg_len,
    gathered,
    w_proj_hbm,
    w_qkv_hbm,
    w_attn_hbm,
    w_out_hbm,
    cot_all,
    slide_of,
    order_of,
    d_pooled,
    d_embed,
    context,
    slide_rows,
    pooled_pair,
    w_proj,
    w_qkv,
    w_attn,
    w_out,
    d_qkv,
    sems,
):
    copies = [
        pltpu.make_async_copy(src, dst, sems.at[i])
        for i, (src, dst) in enumerate(
            [(w_proj_hbm, w_proj), (w_qkv_hbm, w_qkv), (w_attn_hbm, w_attn), (w_out_hbm, w_out)]
        )
    ]
    for copy in copies:
        copy.start()
    tiles = slide_of.shape[1]
    half = w_proj.shape[0] // 2
    width = w_proj.shape[1]
    head = width // HEADS

    row = lax.broadcasted_iota(jnp.int32, (tiles, 2 * tiles), 0)
    col = lax.broadcasted_iota(jnp.int32, (tiles, 2 * tiles), 1)
    first = (row // 4) * 8 + row % 4
    every = gathered[...]
    left = dot_nn((col == first).astype(F4).astype(BF), every).astype(BF)
    right = dot_nn((col == first + 4).astype(F4).astype(BF), every).astype(BF)
    pooled_pair[:, :128] = left[:, half:]
    pooled_pair[:, 128:] = right[:, half:]

    slide = slide_of[...].astype(F4)
    order = order_of[...].astype(F4)
    weight = jnp.zeros((tiles, tiles), F4)
    for branch in range(3):
        length = seg_len[branch].astype(F4)
        block = jnp.floor((order + 0.5) / length)
        dilation = float(2**branch)
        phase = order - dilation * jnp.floor(order * (1.0 / dilation))
        code = jnp.broadcast_to((slide * 64.0 + block) * 4.0 + phase, (tiles, tiles))
        weight = weight + (code == code.T).astype(F4)
    slide_col = jnp.broadcast_to(slide, (tiles, tiles)).T
    lane = lax.broadcasted_iota(jnp.int32, (tiles, 16), 1).astype(F4)
    member = (slide_col[:, :16] == lane).astype(F4).astype(BF)
    cot_high, cot_low = halves(cot_all[...])
    d_attended = dot_nn(member, cot_high) + dot_nn(member, cot_low)

    copies[0].wait()
    rows = (dot_nn(left[:, :half], w_proj[:half, :]) + dot_nn(right[:, :half], w_proj[half:, :])).astype(BF)
    slide_rows[...] = rows
    copies[1].wait()
    qkv = dot_nn(rows, w_qkv[...]).astype(BF)
    copies[2].wait()
    d_context = dot_nt(d_attended.astype(BF), w_attn[...]).astype(BF)

    scale = 1.0 / math.sqrt(head)
    sums = {}

    def accumulate(name, start, value):
        for offset in range(0, value.shape[1], 128):
            key = (name, (start + offset) // 128)
            piece = value[:, offset : offset + 128]
            sums[key] = sums[key] + piece if key in sums else piece

    for index in range(HEADS):
        low = index * head
        start = low // 128 * 128
        stop = -(-(low + head) // 128) * 128
        place_in = lax.broadcasted_iota(jnp.int32, (1, stop - start), 1) + start
        mask = ((place_in >= low) & (place_in < low + head)).astype(F4)
        mask_bf = mask.astype(BF)
        query = qkv[:, start:stop] * mask_bf
        key_rows = qkv[:, width + start : width + stop]
        value_rows = qkv[:, 2 * width + start : 2 * width + stop]
        d_out = d_context[:, start:stop] * mask_bf
        scores = jnp.where(weight > 0.0, dot_nt(query, key_rows) * scale, -1e30)
        numerator = weight * jnp.exp(scores - jnp.max(scores, axis=1, keepdims=True))
        share = numerator * (1.0 / jnp.sum(numerator, axis=1, keepdims=True))
        d_share = dot_nt(d_out, value_rows)
        d_scores = share * (d_share - jnp.sum(share * d_share, axis=1, keepdims=True)) * scale
        share = share.astype(BF)
        d_scores = d_scores.astype(BF)
        accumulate("context", start, dot_nn(share, value_rows) * mask)
        accumulate("query", start, dot_nn(d_scores, key_rows) * mask)
        accumulate("key", start, dot_tn(d_scores, query))
        accumulate("value", start, dot_tn(share, d_out))
    for tile in range(width // 128):
        context[:, 128 * tile : 128 * (tile + 1)] = sums["context", tile]
        for part, name in enumerate(("query", "key", "value")):
            at = part * width + 128 * tile
            d_qkv[:, at : at + 128] = sums[name, tile].astype(BF)

    d_slide = d_attended + dot_nt(d_qkv[...], w_qkv[...])
    d_embed[...] = dot_nt(d_slide.astype(BF), w_proj[...])
    copies[3].wait()
    eight = d_embed[pl.ds(pl.multiple_of(place[1] // 2 * 8, 8), 8), :]
    high, low = halves(eight)
    back = dot_nt(high, w_out[...]) + dot_nt(low, w_out[...])
    d_pooled[...] = jnp.where(place[1] % 2 == 0, back[:4, :], back[4:, :]) * (1.0 / 256.0)


def attention(place, seg_len, gathered, w_proj, w_qkv, w_attn, w_out, cot_all, slide_of, order_of):
    tiles = slide_of.shape[1]
    width, slide_width = w_proj.shape
    hidden = w_out.shape[0]
    smem = pl.BlockSpec(memory_space=pltpu.SMEM)
    vmem = pl.BlockSpec(memory_space=pltpu.VMEM)
    hbm = pl.BlockSpec(memory_space=pl.ANY)
    return pl.pallas_call(
        attention_kernel,
        in_specs=[smem, smem, vmem, hbm, hbm, hbm, hbm, vmem, vmem, vmem],
        out_shape=[
            jax.ShapeDtypeStruct((4, hidden), F4),
            jax.ShapeDtypeStruct((tiles, width), F4),
            jax.ShapeDtypeStruct((tiles, slide_width), F4),
            jax.ShapeDtypeStruct((tiles, slide_width), BF),
            jax.ShapeDtypeStruct((tiles, 256), BF),
        ],
        scratch_shapes=[
            pltpu.VMEM(w_proj.shape, BF),
            pltpu.VMEM(w_qkv.shape, BF),
            pltpu.VMEM(w_attn.shape, BF),
            pltpu.VMEM(w_out.shape, BF),
            pltpu.VMEM((tiles, 3 * slide_width), BF),
            pltpu.SemaphoreType.DMA((4,)),
        ],
        compiler_params=pltpu.CompilerParams(vmem_limit_bytes=40 * MIB),
        name="attention",
    )(place, seg_len, gathered, w_proj, w_qkv, w_attn, w_out, cot_all, slide_of, order_of)


def outputs_kernel(place, context, slide_rows, w_attn, slide_of, counts, pooled_pair, d_embed, slide_embed, grad_out):
    tiles = slide_of.shape[1]
    high, low = halves(context[...])
    attended = slide_rows[...].astype(F4) + dot_nn(high, w_attn[...]) + dot_nn(low, w_attn[...])
    group = lax.broadcasted_iota(jnp.int32, (16, tiles), 0)
    member = (slide_of[...] == group).astype(F4).astype(BF)
    high, low = halves(attended)
    sums = (dot_nn(member, high) + dot_nn(member, low)) / counts[...].astype(F4)
    own = sums[0:4, :]
    for index in range(1, 4):
        own = jnp.where(place[0] == index, sums[4 * index : 4 * index + 4, :], own)
    slide_embed[...] = own
    high, low = halves(d_embed[...])
    pair = pooled_pair[...]
    both = dot_tn(pair, high) + dot_tn(pair, low)
    rows = grad_out.shape[0]
    grad_out[...] = both[:rows, :] + both[128 : 128 + rows, :]


def outputs(place, context, slide_rows, w_attn, slide_of, counts, pooled_pair, d_embed, rows):
    slide_width = w_attn.shape[0]
    width = d_embed.shape[1]
    return pl.pallas_call(
        outputs_kernel,
        in_specs=[pl.BlockSpec(memory_space=pltpu.SMEM)] + [pl.BlockSpec(memory_space=pltpu.VMEM)] * 7,
        out_shape=[jax.ShapeDtypeStruct((4, slide_width), F4), jax.ShapeDtypeStruct((rows, width), F4)],
        compiler_params=pltpu.CompilerParams(vmem_limit_bytes=16 * MIB),
        cost_estimate=pl.CostEstimate(flops=1_000_000_000, bytes_accessed=4_000_000, transcendentals=0),
        name="outputs",
    )(place, context, slide_rows, w_attn, slide_of, counts, pooled_pair, d_embed)


def grad_kernel(normed_t, slope, d_pooled, send, keep):
    tile_count = d_pooled.shape[0]
    patches = slope.shape[0] // tile_count
    parts = []
    for tile in range(tile_count):
        rate = slope[pl.ds(tile * patches, patches), :].astype(F4)
        parts.append((rate * d_pooled[pl.ds(tile, 1), :]).astype(BF))
    d_preact = jnp.concatenate(parts, axis=0)
    rows = send.shape[0]
    send[...] = dot_nn(normed_t[:rows, :], d_preact).astype(BF)
    keep[...] = dot_nn(normed_t[rows:, :], d_preact).astype(BF)


def grad_half(normed_t, slope, d_pooled, which, block=256):
    width, tokens = normed_t.shape
    hidden = slope.shape[1] // 2
    steps = hidden // block
    out = pl.BlockSpec((width // 2, block), lambda j: (0, j))
    return pl.pallas_call(
        grad_kernel,
        grid=(steps,),
        in_specs=[
            pl.BlockSpec((width, tokens), lambda j: (0, 0)),
            pl.BlockSpec((tokens, block), lambda j: (0, j + which * steps)),
            pl.BlockSpec((d_pooled.shape[0], block), lambda j: (0, j + which * steps)),
        ],
        out_specs=[out, out],
        out_shape=[jax.ShapeDtypeStruct((width // 2, hidden), BF)] * 2,
        compiler_params=pltpu.CompilerParams(vmem_limit_bytes=24 * MIB),
        cost_estimate=pl.CostEstimate(flops=2 * width * tokens * hidden, bytes_accessed=7_000_000, transcendentals=0),
        name="grad_half",
    )(normed_t, slope, d_pooled)


def add_pair_kernel(keep, received, *outs):
    rows = outs[0].shape[0]
    for index, out in enumerate(outs):
        at = pl.ds(index * rows, rows)
        out[...] = (keep[at, :].astype(F4) + received[at, :].astype(F4)).astype(BF)


def add_pair(keep, received):
    rows, columns = keep.shape
    return pl.pallas_call(
        add_pair_kernel,
        out_shape=[jax.ShapeDtypeStruct((rows // 4, columns), BF)] * 4,
        compiler_params=pltpu.CompilerParams(vmem_limit_bytes=16 * MIB),
        name="add_pair",
    )(keep, received)


def add_four_kernel(one, two, three, four, *outs):
    rows = outs[0].shape[0]
    for index, out in enumerate(outs):
        at = pl.ds(index * rows, rows)
        total = (one[at, :].astype(F4) + two[at, :].astype(F4)) + (three[at, :].astype(F4) + four[at, :].astype(F4))
        out[...] = total.astype(BF)


def add_four(parts):
    rows, columns = parts[0].shape
    return pl.pallas_call(
        add_four_kernel,
        out_shape=[jax.ShapeDtypeStruct((rows // 4, columns), BF)] * 4,
        compiler_params=pltpu.CompilerParams(vmem_limit_bytes=16 * MIB),
        name="add_four",
    )(*parts)


def finish_kernel(*refs):
    out = refs[-1]
    half = out.shape[1] // 2
    for side in range(2):
        one, two, three, four = [ref[...].astype(F4) for ref in refs[4 * side : 4 * side + 4]]
        out[:, side * half : (side + 1) * half] = (one + two) + (three + four)


def finish(parts):
    rows, columns = parts[0].shape
    return pl.pallas_call(
        finish_kernel,
        out_shape=jax.ShapeDtypeStruct((rows, 2 * columns), F4),
        name="finish",
    )(*parts)


def moved(value, dz, dx, dc):
    pairs = []
    for z in range(4):
        for x in range(4):
            for c in range(2):
                pairs.append(((z * 4 + x) * 2 + c, ((z + dz) % 4 * 4 + (x + dx) % 4) * 2 + (c + dc) % 2))
    return lax.ppermute(value, "tile", pairs)


def on_device(
    tiles,
    w_in,
    w_out,
    w_proj,
    w_qkv,
    w_attn_out,
    slide_of_tile,
    order_of_tile,
    slide_counts,
    seg_len,
    slide_cot,
):
    tile_count, patches, width = tiles.shape
    hidden = w_in.shape[1]
    peers = 32
    flat = tiles.reshape(tile_count * patches, width)
    tile_pos = lax.axis_index("tile")
    slide_pos = lax.axis_index("slide")
    place = jnp.stack([slide_pos, tile_pos]).astype(jnp.int32)
    counts = slide_counts.reshape(-1, 1)
    slide_of = slide_of_tile.reshape(1, -1)
    order_of = order_of_tile.reshape(1, -1)

    block = jnp.arange(peers, dtype=jnp.int32)
    z, x, c = block // 8, block // 2 % 4, block % 2
    dz = (z - tile_pos // 8) % 4
    dx = (x - tile_pos // 2 % 4) % 4
    stay = (c == tile_pos % 2).astype(jnp.int32)
    place_a = (stay * 16 + dx * 4 + dz).astype(jnp.int32)
    place_b = (stay * 16 + dz * 4 + dx).astype(jnp.int32)

    slope, pooled, shared, token_mean = forward(flat, w_in, w_out, slide_cot, tile_count)
    parts = [shared] + [
        lax.ppermute(shared, "slide", [(i, (i + k) % 4) for i in range(4)]) for k in (1, 2, 3)
    ]
    order_a, order_b = transposed(flat, place_a, place_b, patches)
    slices = pooled.reshape(2 * tile_count, peers, hidden // peers).transpose(1, 0, 2)
    slices = jnp.pad(slices.reshape(peers * 2 * tile_count, -1), ((0, 0), (0, 128 - hidden // peers)))
    mine, cot_all = embed(place, parts, token_mean, counts, slices, peers)
    gathered = lax.all_to_all(
        mine.reshape(peers, 8, -1), "tile", split_axis=0, concat_axis=0, tiled=True
    ).reshape(peers * 8, -1)
    d_pooled, d_embed, context, slide_rows, pooled_pair = attention(
        place, seg_len, gathered, w_proj, w_qkv, w_attn_out, w_out, cot_all, slide_of, order_of
    )
    send_a, keep_a = grad_half(order_a, slope, d_pooled, 0)
    send_b, keep_b = grad_half(order_b, slope, d_pooled, 1)
    a = add_pair(keep_a, moved(send_a, 0, 0, 1))
    b = add_pair(keep_b, moved(send_b, 0, 0, 1))
    a = add_four([a[0]] + [moved(a[k], 0, k, 0) for k in (1, 2, 3)])
    b = add_four([b[0]] + [moved(b[k], k, 0, 0) for k in (1, 2, 3)])
    slide_embed, grad_out = outputs(
        place, context, slide_rows, w_attn_out, slide_of, counts, pooled_pair, d_embed, hidden // peers
    )
    a = [a[0]] + [moved(a[k], k, 0, 0) for k in (1, 2, 3)]
    b = [b[0]] + [moved(b[k], 0, k, 0) for k in (1, 2, 3)]
    return (slide_embed, finish(a + b), grad_out)


def solution(mesh):
    placed = (
        P("tile", None, None),
        P(None, "slide"),
        P("slide", None),
        P(),
        P(),
        P(),
        P(),
        P(),
        P(),
        P(),
        P("slide", None),
    )
    return jax.shard_map(
        on_device,
        mesh=mesh,
        in_specs=placed,
        out_specs=(P("slide", None), P("tile", "slide"), P(("slide", "tile"), None)),
        check_vma=False,
    )
```

```python
import math

import jax
import jax.numpy as jnp
from jax import lax
from jax.experimental import pallas as pl
from jax.experimental.pallas import tpu as pltpu
from jax.sharding import PartitionSpec as P

HEADS = 16
EPSILON = 1e-06
MIB = 1 << 20
BF = jnp.bfloat16
F4 = jnp.float32


def dot_nn(a, b):
    return lax.dot_general(a, b, (((1,), (0,)), ((), ())), preferred_element_type=F4)


def dot_nt(a, b):
    return lax.dot_general(a, b, (((1,), (1,)), ((), ())), preferred_element_type=F4)


def dot_tn(a, b):
    return lax.dot_general(a, b, (((0,), (0,)), ((), ())), preferred_element_type=F4)


def halves(value):
    high = value.astype(BF)
    return high, (value - high.astype(F4)).astype(BF)


def standardise(values):
    width = values.shape[1]
    centre = jnp.sum(values, axis=1, keepdims=True) * (1.0 / width)
    shifted = values - centre
    spread = jnp.sum(shifted * shifted, axis=1, keepdims=True) * (1.0 / width)
    return shifted * lax.rsqrt(spread + EPSILON)


def gelu_pair(a):
    bell = jnp.exp(a * a * -0.5)
    t = 1.0 / (1.0 + jnp.abs(a) * (0.3275911 * 0.7071067811865476))
    series = t * (0.127414796 + t * (-0.142248368 + t * (0.7107068705 + t * (-0.7265760135 + t * 0.5307027145))))
    tail = series * bell
    phi = jnp.where(a < 0.0, tail, 1.0 - tail)
    return a * phi, phi + a * (bell * 0.3989422804014327)


def from_hbm(value):
    return pltpu.with_memory_space_constraint(value, pltpu.HBM)


def from_vmem(value):
    return pltpu.with_memory_space_constraint(value, pltpu.VMEM)


ANY = pl.BlockSpec(memory_space=pl.ANY)
SMEM = pl.BlockSpec(memory_space=pltpu.SMEM)
VMEM = pl.BlockSpec(memory_space=pltpu.VMEM)


def forward_kernel(
    place, tiles_hbm, w_in, w_out, cot, slope_send, slope_keep, pooled, shared, token_mean, normed_hbm, tiles, normed, total, sems
):
    step = pl.program_id(0)
    steps = pl.num_programs(0)
    tile_count = token_mean.shape[0]
    patches = tiles.shape[0] // tile_count
    pieces = [pl.ds(tile * patches, patches) for tile in range(tile_count)]
    out_copies = [
        pltpu.make_async_copy(normed.at[rows], normed_hbm.at[rows], sems.at[tile_count + tile])
        for tile, rows in enumerate(pieces)
    ]

    @pl.when(step == 0)
    def _():
        in_copies = [
            pltpu.make_async_copy(tiles_hbm.at[rows], tiles.at[rows], sems.at[tile]) for tile, rows in enumerate(pieces)
        ]
        for copy in in_copies:
            copy.start()
        for tile, rows in enumerate(pieces):
            in_copies[tile].wait()
            values = tiles[rows, :].astype(F4)
            token_mean[pl.ds(tile, 1), :] = jnp.sum(values, axis=0, keepdims=True) * (1.0 / patches)
            normed[rows, :] = standardise(values).astype(BF)
            out_copies[tile].start()
        total[...] = jnp.zeros_like(total)

    def work(slope):
        means = []
        for rows in pieces:
            value, rate = gelu_pair(dot_nn(normed[rows, :], w_in[...]))
            slope[rows, :] = rate.astype(BF)
            means.append(jnp.sum(value, axis=0, keepdims=True) * (1.0 / patches))
        high, low = halves(jnp.concatenate(means, axis=0))
        both = jnp.concatenate([high, low], axis=0)
        pooled[...] = both
        total[...] += dot_nn(both, w_out[...])

    @pl.when(step < steps // 2)
    def _():
        work(slope_send)

    @pl.when(step >= steps // 2)
    def _():
        work(slope_keep)

    @pl.when(step == steps - 1)
    def _():
        width = total.shape[1]
        shared[:, :width] = total[:tile_count, :] + total[tile_count:, :]
        shared[:, width:] = cot[...]
        for copy in out_copies:
            copy.wait()


def forward(place, tiles, w_in, w_out, cot, tile_count):
    tokens, width = tiles.shape
    hidden = w_in.shape[1]
    block = 256
    steps = hidden // block
    slide_width = cot.shape[1]

    def at(j, place):
        return (j + steps // 2 * (1 - place[2])) % steps

    return pl.pallas_call(
        forward_kernel,
        grid_spec=pltpu.PrefetchScalarGridSpec(
            num_scalar_prefetch=1,
            grid=(steps,),
            in_specs=[
                ANY,
                pl.BlockSpec((width, block), lambda j, place: (0, at(j, place))),
                pl.BlockSpec((block, width), lambda j, place: (at(j, place), 0)),
                pl.BlockSpec((tile_count, slide_width), lambda j, place: (0, 0)),
            ],
            out_specs=[
                pl.BlockSpec((tokens, block), lambda j, place: (0, jnp.minimum(j, steps // 2 - 1))),
                pl.BlockSpec((tokens, block), lambda j, place: (0, jnp.maximum(j - steps // 2, 0))),
                pl.BlockSpec((2 * tile_count, block), lambda j, place: (0, at(j, place))),
                pl.BlockSpec((tile_count, width + slide_width), lambda j, place: (0, 0)),
                pl.BlockSpec((tile_count, width), lambda j, place: (0, 0)),
                ANY,
            ],
            scratch_shapes=[
                pltpu.VMEM((tokens, width), BF),
                pltpu.VMEM((tokens, width), BF),
                pltpu.VMEM((2 * tile_count, width), F4),
                pltpu.SemaphoreType.DMA((2 * tile_count,)),
            ],
        ),
        out_shape=[
            pltpu.HBM((tokens, hidden // 2), BF),
            pltpu.HBM((tokens, hidden // 2), BF),
            jax.ShapeDtypeStruct((2 * tile_count, hidden), BF),
            jax.ShapeDtypeStruct((tile_count, width + slide_width), F4),
            jax.ShapeDtypeStruct((tile_count, width), F4),
            pltpu.HBM((tokens, width), BF),
        ],
        compiler_params=pltpu.CompilerParams(vmem_limit_bytes=32 * MIB),
        name="forward",
    )(place, from_hbm(tiles), from_hbm(w_in), from_hbm(w_out), cot)


def transpose_kernel(after, normed, out):
    out[...] = normed[...].T


def transposed(normed, after, patches):
    tokens, width = normed.shape
    return pl.pallas_call(
        transpose_kernel,
        grid=(tokens // patches,),
        in_specs=[ANY, pl.BlockSpec((patches, width), lambda i: (i, 0))],
        out_specs=pl.BlockSpec((width, patches), lambda i: (0, i)),
        out_shape=pltpu.HBM((width, tokens), BF),
        compiler_params=pltpu.CompilerParams(vmem_limit_bytes=16 * MIB),
        cost_estimate=pl.CostEstimate(flops=20_000_000, bytes_accessed=9_000_000, transcendentals=0),
        name="transposed",
    )(after, from_hbm(normed))


def embed_kernel(
    place, own, one, two, three, token_mean, counts, pooled, normed_in, slope_in, out, cot_all, normed_out, slope_out
):
    width = token_mean.shape[1]
    half = width // 2
    total = (own[:, :width] + two[:, :width]) + (one[:, :width] + three[:, :width])
    embedding = total + token_mean[...]
    eight = jnp.concatenate([embedding[:, :half], embedding[:, half:]], axis=0)
    out[:, :half] = jnp.concatenate([eight] * (out.shape[0] // 8), axis=0).astype(BF)
    out[:, half:] = pooled[...]
    parts = [own[:, width:], one[:, width:], two[:, width:], three[:, width:]]
    blocks = []
    for group in range(4):
        back = jnp.bitwise_and(place[0] - group, 3)
        block = parts[0]
        for shift in range(1, 4):
            block = jnp.where(back == shift, parts[shift], block)
        blocks.append(block)
    cot_all[...] = jnp.concatenate(blocks, axis=0) / counts[...].astype(F4)


def embed(place, parts, token_mean, counts, pooled, normed, slope, peers):
    tile_count, width = token_mean.shape
    slide_width = parts[0].shape[1] - width
    return pl.pallas_call(
        embed_kernel,
        in_specs=[SMEM] + [VMEM] * 7 + [ANY] * 2,
        out_specs=[VMEM] * 2 + [ANY] * 2,
        out_shape=[
            jax.ShapeDtypeStruct((peers * 8, width // 2 + 128), BF),
            jax.ShapeDtypeStruct((16, slide_width), F4),
            pltpu.HBM(normed.shape, BF),
            pltpu.HBM(slope.shape, BF),
        ],
        input_output_aliases={8: 2, 9: 3},
        compiler_params=pltpu.CompilerParams(vmem_limit_bytes=8 * MIB),
        name="embed",
    )(place, *parts, token_mean, counts, pooled, from_hbm(normed), from_hbm(slope))


def attention_kernel(
    place,
    seg_len,
    gathered,
    cot_all,
    slide_of,
    order_of,
    w_proj_hbm,
    w_qkv_hbm,
    w_attn_hbm,
    w_out_hbm,
    normed_own,
    normed_other,
    slope_own,
    slope_other,
    d_preact,
    lhs0,
    lhs1,
    lhs2,
    lhs3,
    d_embed,
    context,
    slide_rows,
    pooled_pair,
    slope,
    w_proj,
    w_qkv,
    w_attn,
    w_out,
    sems,
):
    hidden = w_out.shape[0]
    half_rows = pl.ds(pl.multiple_of(place[2] * hidden, hidden), hidden)
    pairs = [(w_proj_hbm, w_proj), (w_qkv_hbm, w_qkv), (w_attn_hbm, w_attn), (w_out_hbm.at[half_rows], w_out)]
    loads = [pltpu.make_async_copy(src, dst, sems.at[34 + i]) for i, (src, dst) in enumerate(pairs)]
    for load in loads:
        load.start()

    tokens = slope_own.shape[0]
    rows_each = lhs0.shape[0] // 4
    core = place[2]
    copies = [
        pltpu.make_async_copy(slope_own, slope.at[pl.ds(0, tokens)], sems.at[0]),
        pltpu.make_async_copy(slope_other, slope.at[pl.ds(tokens, tokens)], sems.at[1]),
    ]
    for chunk, lhs in enumerate((lhs0, lhs1, lhs2, lhs3)):
        for sub in range(4):
            z = (place[3] + jnp.where(core == 0, sub, chunk)) % 4
            x = (place[4] + jnp.where(core == 0, chunk, sub)) % 4
            source = pl.ds(pl.multiple_of((z * 4 + x) * rows_each, 16), rows_each)
            rows = pl.ds(sub * rows_each, rows_each)
            at = 2 + 2 * (4 * chunk + sub)
            copies.append(pltpu.make_async_copy(normed_own.at[source], lhs.at[rows, pl.ds(0, tokens)], sems.at[at]))
            copies.append(
                pltpu.make_async_copy(normed_other.at[source], lhs.at[rows, pl.ds(tokens, tokens)], sems.at[at + 1])
            )
    for copy in copies:
        copy.start()

    tiles = slide_of.shape[1]
    half = w_proj.shape[0] // 2
    width = w_proj.shape[1]
    head = width // HEADS

    row = lax.broadcasted_iota(jnp.int32, (tiles, 2 * tiles), 0)
    col = lax.broadcasted_iota(jnp.int32, (tiles, 2 * tiles), 1)
    first = (row // 4) * 8 + row % 4
    every = gathered[...]
    left = dot_nn((col == first).astype(F4).astype(BF), every).astype(BF)
    right = dot_nn((col == first + 4).astype(F4).astype(BF), every).astype(BF)
    pooled_pair[:, :128] = left[:, half:]
    pooled_pair[:, 128:] = right[:, half:]
    loads[0].wait()
    rows = (dot_nn(left[:, :half], w_proj[:half, :]) + dot_nn(right[:, :half], w_proj[half:, :])).astype(BF)
    slide_rows[...] = rows
    loads[1].wait()
    qkv = dot_nn(rows, w_qkv[...]).astype(BF)

    slide = slide_of[...].astype(F4)
    order = order_of[...].astype(F4)
    weight = jnp.zeros((tiles, tiles), F4)
    for branch in range(3):
        length = seg_len[branch].astype(F4)
        block = jnp.floor((order + 0.5) / length)
        dilation = float(2**branch)
        phase = order - dilation * jnp.floor(order * (1.0 / dilation))
        code = jnp.broadcast_to((slide * 64.0 + block) * 4.0 + phase, (tiles, tiles))
        weight = weight + (code == code.T).astype(F4)
    slide_col = jnp.broadcast_to(slide, (tiles, tiles)).T
    lane = lax.broadcasted_iota(jnp.int32, (tiles, 16), 1).astype(F4)
    member = (slide_col[:, :16] == lane).astype(F4).astype(BF)
    cot_high, cot_low = halves(cot_all[...])
    d_attended = dot_nn(member, cot_high) + dot_nn(member, cot_low)
    loads[2].wait()
    d_context = dot_nt(d_attended.astype(BF), w_attn[...]).astype(BF)

    scale = 1.0 / math.sqrt(head)
    group_heads = HEADS // 2
    group_width = group_heads * head
    lanes = lax.broadcasted_iota(jnp.int32, (1, group_width), 1)
    masks = [((lanes >= h * head) & (lanes < (h + 1) * head)).astype(F4).astype(BF) for h in range(group_heads)]

    def stacked(value):
        return jnp.concatenate([value * mask for mask in masks], axis=0)

    def beside(parts):
        return jnp.concatenate(parts, axis=1)

    grads = {}
    for group in range(2):
        start = group * group_width
        query = qkv[:, start : start + group_width]
        key_rows = qkv[:, width + start : width + start + group_width]
        value_rows = qkv[:, 2 * width + start : 2 * width + start + group_width]
        d_out = d_context[:, start : start + group_width]
        query_stack, d_out_stack = stacked(query), stacked(d_out)
        scores = dot_nt(query_stack, key_rows)
        d_share = dot_nt(d_out_stack, value_rows)
        shares, d_scores = [], []
        for h in range(group_heads):
            at = slice(h * tiles, (h + 1) * tiles)
            score = jnp.where(weight > 0.0, scores[at] * scale, -1e30)
            numerator = weight * jnp.exp(score - jnp.max(score, axis=1, keepdims=True))
            share = numerator * (1.0 / jnp.sum(numerator, axis=1, keepdims=True))
            slant = share * d_share[at]
            d_score = (slant - share * jnp.sum(slant, axis=1, keepdims=True)) * scale
            shares.append(share.astype(BF))
            d_scores.append(d_score.astype(BF))
        context[:, start : start + group_width] = dot_nn(beside(shares), stacked(value_rows))
        grads["query", group] = dot_nn(beside(d_scores), stacked(key_rows))
        grads["key", group] = dot_nn(beside([part.T for part in d_scores]), query_stack)
        grads["value", group] = dot_nn(beside([part.T for part in shares]), d_out_stack)
    d_qkv = beside([grads[name, group].astype(BF) for name in ("query", "key", "value") for group in range(2)])

    d_slide = d_attended + dot_nt(d_qkv, w_qkv[...])
    d_embed[...] = dot_nt(d_slide.astype(BF), w_proj[...])
    eight = d_embed[pl.ds(pl.multiple_of(place[1] // 2 * 8, 8), 8), :]
    high, low = halves(eight)
    loads[3].wait()
    back = dot_nt(jnp.concatenate([high, low], axis=0), w_out[...])
    back = back[:8, :] + back[8:, :]
    back = jnp.where(core == 0, back, jnp.concatenate([back[4:, :], back[:4, :]], axis=0)) * (4.0 / tokens)
    for copy in copies:
        copy.wait()
    patches = tokens // 4
    for tile in range(8):
        at = pl.ds(tile * patches, patches)
        d_preact[at, :] = (slope[at, :].astype(F4) * back[tile : tile + 1, :]).astype(BF)


def attention(place, seg_len, gathered, weights, cot_all, slide_of, order_of, normed, slopes):
    w_proj, w_qkv, w_attn, w_out = weights
    tiles = slide_of.shape[1]
    width, slide_width = w_proj.shape
    hidden = w_out.shape[0] // 2
    tokens = slopes[0].shape[0]
    return pl.pallas_call(
        attention_kernel,
        in_specs=[SMEM, SMEM] + [VMEM] * 4 + [ANY] * 8,
        out_specs=[VMEM] * 9,
        out_shape=[
            pltpu.VMEM((2 * tokens, hidden), BF),
            *[pltpu.VMEM((width // 4, 2 * tokens), BF)] * 4,
            jax.ShapeDtypeStruct((tiles, width), F4),
            jax.ShapeDtypeStruct((tiles, slide_width), F4),
            jax.ShapeDtypeStruct((tiles, slide_width), BF),
            jax.ShapeDtypeStruct((tiles, 256), BF),
        ],
        scratch_shapes=[
            pltpu.VMEM((2 * tokens, hidden), BF),
            pltpu.VMEM(w_proj.shape, BF),
            pltpu.VMEM(w_qkv.shape, BF),
            pltpu.VMEM(w_attn.shape, BF),
            pltpu.VMEM((hidden, width), BF),
            pltpu.SemaphoreType.DMA((38,)),
        ],
        compiler_params=pltpu.CompilerParams(vmem_limit_bytes=24 * MIB),
        name="attention",
    )(
        place,
        seg_len,
        gathered,
        cot_all,
        slide_of,
        order_of,
        *[from_hbm(value) for value in (*weights, *normed, *slopes)],
    )


def outputs_kernel(place, context, slide_rows, w_attn, slide_of, counts, pooled_pair, d_embed, slide_embed, grad_out):
    tiles = slide_of.shape[1]
    high, low = halves(context[...])
    attended = slide_rows[...].astype(F4) + dot_nn(high, w_attn[...]) + dot_nn(low, w_attn[...])
    group = lax.broadcasted_iota(jnp.int32, (16, tiles), 0)
    member = (slide_of[...] == group).astype(F4).astype(BF)
    high, low = halves(attended)
    sums = (dot_nn(member, high) + dot_nn(member, low)) / counts[...].astype(F4)
    own = sums[0:4, :]
    for index in range(1, 4):
        own = jnp.where(place[0] == index, sums[4 * index : 4 * index + 4, :], own)
    slide_embed[...] = own
    high, low = halves(d_embed[...])
    pair = pooled_pair[...]
    both = dot_tn(pair, high) + dot_tn(pair, low)
    rows = grad_out.shape[0]
    grad_out[...] = both[:rows, :] + both[128 : 128 + rows, :]


def outputs(place, context, slide_rows, w_attn, slide_of, counts, pooled_pair, d_embed, rows):
    slide_width = w_attn.shape[0]
    width = d_embed.shape[1]
    return pl.pallas_call(
        outputs_kernel,
        in_specs=[pl.BlockSpec(memory_space=pltpu.SMEM)] + [pl.BlockSpec(memory_space=pltpu.VMEM)] * 7,
        out_shape=[jax.ShapeDtypeStruct((4, slide_width), F4), jax.ShapeDtypeStruct((rows, width), F4)],
        compiler_params=pltpu.CompilerParams(vmem_limit_bytes=16 * MIB),
        cost_estimate=pl.CostEstimate(flops=1000, bytes_accessed=1000, transcendentals=0),
        name="outputs",
    )(place, context, slide_rows, w_attn, slide_of, counts, pooled_pair, d_embed)


def grad_kernel(lhs, d_preact, out):
    out[...] = dot_nn(lhs[...], d_preact[...]).astype(BF)


def grad_chunk(lhs, d_preact):
    rows, tokens = lhs.shape
    hidden = d_preact.shape[1]
    return pl.pallas_call(
        grad_kernel,
        in_specs=[VMEM] * 2,
        out_specs=VMEM,
        out_shape=jax.ShapeDtypeStruct((rows, hidden), BF),
        compiler_params=pltpu.CompilerParams(vmem_limit_bytes=16 * MIB),
        cost_estimate=pl.CostEstimate(flops=1000, bytes_accessed=1000, transcendentals=0),
        name="grad_chunk",
    )(from_vmem(lhs), from_vmem(d_preact))


def add_four_kernel(one, two, three, four, after, *outs):
    rows = outs[0].shape[0]
    for index, out in enumerate(outs):
        at = pl.ds(index * rows, rows)
        total = (one[at, :].astype(F4) + two[at, :].astype(F4)) + (three[at, :].astype(F4) + four[at, :].astype(F4))
        out[...] = total.astype(BF)


def add_four(parts, after):
    rows, columns = parts[0].shape
    return pl.pallas_call(
        add_four_kernel,
        in_specs=[VMEM] * 4 + [ANY],
        out_shape=[jax.ShapeDtypeStruct((rows // 4, columns), BF)] * 4,
        compiler_params=pltpu.CompilerParams(vmem_limit_bytes=8 * MIB),
        name="add_four",
    )(*parts, after)


def split_kernel(place, one, two, three, four, keep, send):
    total = (one[...].astype(F4) + two[...].astype(F4)) + (three[...].astype(F4) + four[...].astype(F4))
    rows = keep.shape[0]
    top, bottom = total[:rows, :], total[rows:, :]
    keep[...] = jnp.where(place[2] == 0, top, bottom)
    send[...] = jnp.where(place[2] == 0, bottom, top)


def split(place, parts):
    rows, columns = parts[0].shape
    return pl.pallas_call(
        split_kernel,
        in_specs=[SMEM] + [VMEM] * 4,
        out_shape=[jax.ShapeDtypeStruct((rows // 2, columns), F4)] * 2,
        compiler_params=pltpu.CompilerParams(vmem_limit_bytes=8 * MIB),
        name="split",
    )(place, *parts)


def finish_kernel(place, keep, received, out):
    half = out.shape[1] // 2
    first = place[2] == 0
    out[:, :half] = jnp.where(first, keep[...], received[...])
    out[:, half:] = jnp.where(first, received[...], keep[...])


def finish(place, keep, received):
    rows, columns = keep.shape
    return pl.pallas_call(
        finish_kernel,
        in_specs=[SMEM] + [VMEM] * 2,
        out_shape=jax.ShapeDtypeStruct((rows, 2 * columns), F4),
        compiler_params=pltpu.CompilerParams(vmem_limit_bytes=8 * MIB),
        name="finish",
    )(place, keep, received)


def moved(value, step):
    pairs = []
    for z in range(4):
        for x in range(4):
            for c in range(2):
                to_z, to_x, to_c = step(z, x, c)
                pairs.append(((z * 4 + x) * 2 + c, (to_z % 4 * 4 + to_x % 4) * 2 + to_c % 2))
    return lax.ppermute(value, "tile", pairs)


def other_core(value):
    return moved(value, lambda z, x, c: (z, x, c + 1))


def first_axis(value, k):
    return moved(value, lambda z, x, c: (z, x + k, c) if c == 0 else (z + k, x, c))


def second_axis(value, k):
    return moved(value, lambda z, x, c: (z + k, x, c) if c == 0 else (z, x + k, c))


def on_device(
    tiles,
    w_in,
    w_out,
    w_proj,
    w_qkv,
    w_attn_out,
    slide_of_tile,
    order_of_tile,
    slide_counts,
    seg_len,
    slide_cot,
):
    tile_count, patches, width = tiles.shape
    hidden = w_in.shape[1]
    peers = 32
    flat = tiles.reshape(tile_count * patches, width)
    tile_pos = lax.axis_index("tile")
    slide_pos = lax.axis_index("slide")
    place = jnp.stack([slide_pos, tile_pos, tile_pos % 2, tile_pos // 8, tile_pos // 2 % 4]).astype(jnp.int32)
    counts = slide_counts.reshape(-1, 1)
    slide_of = slide_of_tile.reshape(1, -1)
    order_of = order_of_tile.reshape(1, -1)

    slope_send, slope_keep, pooled, shared, token_mean, normed = forward(place, flat, w_in, w_out, slide_cot, tile_count)
    parts = [shared] + [
        lax.ppermute(shared, "slide", [(i, (i + k) % 4) for i in range(4)]) for k in (1, 2, 3)
    ]
    normed_t = transposed(normed, shared, patches)
    slices = pooled.reshape(2 * tile_count, peers, hidden // peers).transpose(1, 0, 2)
    slices = jnp.pad(slices.reshape(peers * 2 * tile_count, -1), ((0, 0), (0, 128 - hidden // peers)))
    mine, cot_all, normed_t, slope_send = embed(
        place, parts, token_mean, counts, slices, normed_t, slope_send, peers
    )
    gathered = lax.all_to_all(
        mine.reshape(peers, 8, -1), "tile", split_axis=0, concat_axis=0, tiled=True
    ).reshape(peers * 8, -1)
    slope_other, normed_other = other_core(slope_send), other_core(normed_t)
    d_preact, *lhs, d_embed, context, slide_rows, pooled_pair = attention(
        place,
        seg_len,
        gathered,
        (w_proj, w_qkv, w_attn_out, w_out),
        cot_all,
        slide_of,
        order_of,
        (normed_t, normed_other),
        (slope_keep, slope_other),
    )
    chunks = {}
    for k in (2, 1, 3):
        chunks[k] = first_axis(grad_chunk(lhs[k], d_preact), k)
    chunks[0] = grad_chunk(lhs[0], d_preact)
    slide_embed, grad_out = outputs(
        place, context, slide_rows, w_attn_out, slide_of, counts, pooled_pair, d_embed, hidden // peers
    )
    parts = add_four([chunks[k] for k in range(4)], slide_embed)
    parts = [parts[0]] + [second_axis(parts[k], k) for k in (1, 2, 3)]
    keep, send = split(place, parts)
    return (slide_embed, finish(place, keep, other_core(send)), grad_out)


def solution(mesh):
    placed = (
        P("tile", None, None),
        P(None, "slide"),
        P("slide", None),
        P(),
        P(),
        P(),
        P(),
        P(),
        P(),
        P(),
        P("slide", None),
    )
    return jax.shard_map(
        on_device,
        mesh=mesh,
        in_specs=placed,
        out_specs=(P("slide", None), P("tile", "slide"), P(("slide", "tile"), None)),
        check_vma=False,
    )
```

```python
import math

import jax
import jax.numpy as jnp
from jax import lax
from jax.experimental import pallas as pl
from jax.experimental.pallas import tpu as pltpu
from jax.sharding import PartitionSpec as P

HEADS = 16
EPSILON = 1e-06
MIB = 1 << 20
BF = jnp.bfloat16
F4 = jnp.float32


def dot_nn(a, b):
    return lax.dot_general(a, b, (((1,), (0,)), ((), ())), preferred_element_type=F4)


def dot_nt(a, b):
    return lax.dot_general(a, b, (((1,), (1,)), ((), ())), preferred_element_type=F4)


def dot_tn(a, b):
    return lax.dot_general(a, b, (((0,), (0,)), ((), ())), preferred_element_type=F4)


def halves(value):
    high = value.astype(BF)
    return high, (value - high.astype(F4)).astype(BF)


def standardise(values):
    width = values.shape[1]
    centre = jnp.sum(values, axis=1, keepdims=True) * (1.0 / width)
    shifted = values - centre
    spread = jnp.sum(shifted * shifted, axis=1, keepdims=True) * (1.0 / width)
    return shifted * lax.rsqrt(spread + EPSILON)


def gelu_pair(a):
    bell = jnp.exp(a * a * -0.5)
    t = 1.0 / (1.0 + jnp.abs(a) * (0.3275911 * 0.7071067811865476))
    series = t * (0.127414796 + t * (-0.142248368 + t * (0.7107068705 + t * (-0.7265760135 + t * 0.5307027145))))
    tail = series * bell
    phi = jnp.where(a < 0.0, tail, 1.0 - tail)
    return a * phi, phi + a * (bell * 0.3989422804014327)


def from_hbm(value):
    return pltpu.with_memory_space_constraint(value, pltpu.HBM)


def from_vmem(value):
    return pltpu.with_memory_space_constraint(value, pltpu.VMEM)


ANY = pl.BlockSpec(memory_space=pl.ANY)
SMEM = pl.BlockSpec(memory_space=pltpu.SMEM)
VMEM = pl.BlockSpec(memory_space=pltpu.VMEM)


def forward_kernel(
    tiles_hbm,
    w_in_hbm,
    w_out_hbm,
    cot_hbm,
    slope_send,
    slope_keep,
    pooled,
    shared,
    token_mean,
    normed_hbm,
    tiles,
    normed,
    w_in,
    w_out,
    slope,
    total,
    cot,
    tile_sems,
    in_sems,
    out_sems,
    normed_sems,
    slope_sems,
    cot_sem,
):
    core = lax.axis_index("tile") % 2
    tile_count = token_mean.shape[0]
    patches = tiles.shape[0] // tile_count
    steps, _, block = w_in.shape
    half = steps // 2
    pieces = [pl.ds(tile * patches, patches) for tile in range(tile_count)]

    def load_tile(tile):
        return pltpu.make_async_copy(tiles_hbm.at[pieces[tile]], tiles.at[pieces[tile]], tile_sems.at[tile])

    def columns(j):
        return pl.ds(pl.multiple_of((j + half * (1 - core)) % steps * block, block), block)

    def load_in(j):
        return pltpu.make_async_copy(w_in_hbm.at[:, columns(j)], w_in.at[j], in_sems.at[j])

    def load_out(j):
        return pltpu.make_async_copy(w_out_hbm.at[columns(j)], w_out.at[j], out_sems.at[j])

    def store_normed(tile):
        return pltpu.make_async_copy(normed.at[pieces[tile]], normed_hbm.at[pieces[tile]], normed_sems.at[tile])

    def store_slope(j, target):
        at = pl.ds(j % half * block, block)
        return pltpu.make_async_copy(slope.at[j], target.at[:, at], slope_sems.at[j])

    for tile in range(tile_count):
        load_tile(tile).start()
    load_in(0).start()
    load_cot = pltpu.make_async_copy(cot_hbm, cot, cot_sem.at[0])
    load_cot.start()
    for tile in range(tile_count):
        load_tile(tile).wait()
        if tile == 0:
            load_in(1).start()
            load_out(0).start()
        if tile == 2:
            load_in(2).start()
            load_out(1).start()
        values = tiles[pieces[tile], :].astype(F4)
        token_mean[pl.ds(tile, 1), :] = jnp.sum(values, axis=0, keepdims=True) * (1.0 / patches)
        normed[pieces[tile], :] = standardise(values).astype(BF)
        store_normed(tile).start()

    size = 128
    blocks = tiles.shape[0] // size
    per_tile = patches // size
    total[...] = jnp.zeros_like(total)

    def product(item):
        j, part = item // blocks, item % blocks
        if part == 0:
            load_in(j).wait()
            if j + 3 < steps:
                load_in(j + 3).start()
            if j + 2 < steps:
                load_out(j + 2).start()
        return dot_nn(normed[pl.ds(part * size, size), :], w_in[j])

    preact, sums = product(0), []
    for item in range(steps * blocks):
        j, part = item // blocks, item % blocks
        later = product(item + 1) if item + 1 < steps * blocks else None
        value, rate = gelu_pair(preact)
        slope[j, pl.ds(part * size, size), :] = rate.astype(BF)
        sums.append(jnp.sum(value, axis=0, keepdims=True) * (1.0 / patches))
        preact = later
        if part == blocks - 1:
            store_slope(j, slope_send if j < half else slope_keep).start()
            means = [sum(sums[i : i + per_tile]) for i in range(0, blocks, per_tile)]
            high, low = halves(jnp.concatenate(means, axis=0))
            both = jnp.concatenate([high, low], axis=0)
            pooled[:, columns(j)] = both
            load_out(j).wait()
            total[...] += dot_nn(both, w_out[j])
            sums = []
    for j in range(steps):
        store_slope(j, slope_send if j < half else slope_keep).wait()
    width = total.shape[1]
    shared[:, :width] = total[:tile_count, :] + total[tile_count:, :]
    load_cot.wait()
    shared[:, width:] = cot[...]
    for tile in range(tile_count):
        store_normed(tile).wait()


def forward(tiles, w_in, w_out, cot, tile_count):
    tokens, width = tiles.shape
    hidden = w_in.shape[1]
    block = 256
    steps = hidden // block
    slide_width = cot.shape[1]
    return pl.pallas_call(
        forward_kernel,
        in_specs=[ANY] * 4,
        out_specs=[ANY, ANY, VMEM, VMEM, VMEM, ANY],
        out_shape=[
            pltpu.HBM((tokens, hidden // 2), BF),
            pltpu.HBM((tokens, hidden // 2), BF),
            jax.ShapeDtypeStruct((2 * tile_count, hidden), BF),
            jax.ShapeDtypeStruct((tile_count, width + slide_width), F4),
            jax.ShapeDtypeStruct((tile_count, width), F4),
            pltpu.HBM((tokens, width), BF),
        ],
        scratch_shapes=[
            pltpu.VMEM((tokens, width), BF),
            pltpu.VMEM((tokens, width), BF),
            pltpu.VMEM((steps, width, block), BF),
            pltpu.VMEM((steps, block, width), BF),
            pltpu.VMEM((steps, tokens, block), BF),
            pltpu.VMEM((2 * tile_count, width), F4),
            pltpu.VMEM(cot.shape, F4),
            pltpu.SemaphoreType.DMA((tile_count,)),
            pltpu.SemaphoreType.DMA((steps,)),
            pltpu.SemaphoreType.DMA((steps,)),
            pltpu.SemaphoreType.DMA((tile_count,)),
            pltpu.SemaphoreType.DMA((steps,)),
            pltpu.SemaphoreType.DMA((1,)),
        ],
        compiler_params=pltpu.CompilerParams(vmem_limit_bytes=40 * MIB),
        name="forward",
    )(from_hbm(tiles), from_hbm(w_in), from_hbm(w_out), from_hbm(cot))


def transpose_kernel(after, normed, out):
    out[...] = normed[...].T


def transposed(normed, after, patches):
    tokens, width = normed.shape
    return pl.pallas_call(
        transpose_kernel,
        grid=(tokens // patches,),
        in_specs=[ANY, pl.BlockSpec((patches, width), lambda i: (i, 0))],
        out_specs=pl.BlockSpec((width, patches), lambda i: (0, i)),
        out_shape=pltpu.HBM((width, tokens), BF),
        compiler_params=pltpu.CompilerParams(vmem_limit_bytes=16 * MIB),
        cost_estimate=pl.CostEstimate(flops=20_000_000, bytes_accessed=9_000_000, transcendentals=0),
        name="transposed",
    )(after, from_hbm(normed))


def embed_kernel(
    place, own, one, two, three, token_mean, counts, pooled, normed_in, slope_in, out, cot_all, normed_out, slope_out
):
    width = token_mean.shape[1]
    half = width // 2
    total = (own[:, :width] + two[:, :width]) + (one[:, :width] + three[:, :width])
    embedding = total + token_mean[...]
    eight = jnp.concatenate([embedding[:, :half], embedding[:, half:]], axis=0)
    out[:, :half] = jnp.concatenate([eight] * (out.shape[0] // 8), axis=0).astype(BF)
    out[:, half:] = pooled[...]
    parts = [own[:, width:], one[:, width:], two[:, width:], three[:, width:]]
    blocks = []
    for group in range(4):
        back = jnp.bitwise_and(place[0] - group, 3)
        block = parts[0]
        for shift in range(1, 4):
            block = jnp.where(back == shift, parts[shift], block)
        blocks.append(block)
    cot_all[...] = jnp.concatenate(blocks, axis=0) / counts[...].astype(F4)


def embed(place, parts, token_mean, counts, pooled, normed, slope, peers):
    tile_count, width = token_mean.shape
    slide_width = parts[0].shape[1] - width
    return pl.pallas_call(
        embed_kernel,
        in_specs=[SMEM] + [VMEM] * 7 + [ANY] * 2,
        out_specs=[VMEM] * 2 + [ANY] * 2,
        out_shape=[
            jax.ShapeDtypeStruct((peers * 8, width // 2 + 128), BF),
            jax.ShapeDtypeStruct((16, slide_width), F4),
            pltpu.HBM(normed.shape, BF),
            pltpu.HBM(slope.shape, BF),
        ],
        input_output_aliases={8: 2, 9: 3},
        compiler_params=pltpu.CompilerParams(vmem_limit_bytes=8 * MIB),
        name="embed",
    )(place, *parts, token_mean, counts, pooled, from_hbm(normed), from_hbm(slope))


def attention_kernel(
    place,
    seg_len,
    slide_of,
    order_of,
    gathered_hbm,
    cot_hbm,
    w_proj_hbm,
    w_qkv_hbm,
    w_attn_hbm,
    w_out_hbm,
    normed_own,
    normed_other,
    slope_own,
    slope_other,
    d_preact,
    lhs0,
    lhs1,
    lhs2,
    lhs3,
    d_qkv,
    d_direct,
    context,
    slide_rows,
    pooled_pair,
    slope,
    w_proj,
    w_qkv,
    w_attn,
    w_out,
    gathered,
    cot_all,
    sems,
):
    hidden = w_out.shape[0]
    half_rows = pl.ds(pl.multiple_of(place[2] * hidden, hidden), hidden)
    pairs = [(w_proj_hbm, w_proj), (w_qkv_hbm, w_qkv), (w_attn_hbm, w_attn), (w_out_hbm.at[half_rows], w_out)]
    pairs += [(gathered_hbm, gathered), (cot_hbm, cot_all)]
    loads = [pltpu.make_async_copy(src, dst, sems.at[34 + i]) for i, (src, dst) in enumerate(pairs)]
    for index in (4, 0, 5, 2, 1):
        loads[index].start()

    tokens = slope_own.shape[0]
    rows_each = lhs0.shape[0] // 4
    core = place[2]
    copies = [
        pltpu.make_async_copy(slope_own, slope.at[pl.ds(0, tokens)], sems.at[0]),
        pltpu.make_async_copy(slope_other, slope.at[pl.ds(tokens, tokens)], sems.at[1]),
    ]
    for chunk, lhs in enumerate((lhs0, lhs1, lhs2, lhs3)):
        for sub in range(4):
            z = (place[3] + jnp.where(core == 0, sub, chunk)) % 4
            x = (place[4] + jnp.where(core == 0, chunk, sub)) % 4
            source = pl.ds(pl.multiple_of((z * 4 + x) * rows_each, 16), rows_each)
            rows = pl.ds(sub * rows_each, rows_each)
            at = 2 + 2 * (4 * chunk + sub)
            copies.append(pltpu.make_async_copy(normed_own.at[source], lhs.at[rows, pl.ds(0, tokens)], sems.at[at]))
            copies.append(
                pltpu.make_async_copy(normed_other.at[source], lhs.at[rows, pl.ds(tokens, tokens)], sems.at[at + 1])
            )
    tiles = slide_of.shape[1]
    half = w_proj.shape[0] // 2
    width = w_proj.shape[1]
    head = width // HEADS

    slide = slide_of[...].astype(F4)
    order = order_of[...].astype(F4)
    weight = jnp.zeros((tiles, tiles), F4)
    for branch in range(3):
        length = seg_len[branch].astype(F4)
        block = jnp.floor((order + 0.5) / length)
        dilation = float(2**branch)
        phase = order - dilation * jnp.floor(order * (1.0 / dilation))
        code = jnp.broadcast_to((slide * 64.0 + block) * 4.0 + phase, (tiles, tiles))
        weight = weight + (code == code.T).astype(F4)
    slide_col = jnp.broadcast_to(slide, (tiles, tiles)).T
    lane = lax.broadcasted_iota(jnp.int32, (tiles, 16), 1).astype(F4)
    member = (slide_col[:, :16] == lane).astype(F4).astype(BF)
    row = lax.broadcasted_iota(jnp.int32, (tiles, 2 * tiles), 0)
    col = lax.broadcasted_iota(jnp.int32, (tiles, 2 * tiles), 1)
    first = (row // 4) * 8 + row % 4
    loads[4].wait()
    every = gathered[...]
    left = dot_nn((col == first).astype(F4).astype(BF), every).astype(BF)
    right = dot_nn((col == first + 4).astype(F4).astype(BF), every).astype(BF)
    pooled_pair[:, :128] = left[:, half:]
    pooled_pair[:, 128:] = right[:, half:]
    loads[0].wait()
    rows = (dot_nn(left[:, :half], w_proj[:half, :]) + dot_nn(right[:, :half], w_proj[half:, :])).astype(BF)
    slide_rows[...] = rows
    loads[5].wait()
    cot_high, cot_low = halves(cot_all[...])
    d_attended = dot_nn(member, cot_high) + dot_nn(member, cot_low)
    loads[2].wait()
    d_context = dot_nt(d_attended.astype(BF), w_attn[...]).astype(BF)
    loads[1].wait()
    loads[3].start()
    for copy in copies:
        copy.start()
    qkv = dot_nn(rows, w_qkv[...]).astype(BF)

    scale = 1.0 / math.sqrt(head)
    group_heads = HEADS // 2
    group_width = group_heads * head
    lanes = lax.broadcasted_iota(jnp.int32, (1, group_width), 1)
    masks = [((lanes >= h * head) & (lanes < (h + 1) * head)).astype(F4).astype(BF) for h in range(group_heads)]

    def stacked(value):
        return jnp.concatenate([value * mask for mask in masks], axis=0)

    def beside(parts):
        return jnp.concatenate(parts, axis=1)

    grads = {}
    for group in range(2):
        start = group * group_width
        query = qkv[:, start : start + group_width]
        key_rows = qkv[:, width + start : width + start + group_width]
        value_rows = qkv[:, 2 * width + start : 2 * width + start + group_width]
        d_out = d_context[:, start : start + group_width]
        query_stack, d_out_stack = stacked(query), stacked(d_out)
        scores = dot_nt(query_stack, key_rows)
        d_share = dot_nt(d_out_stack, value_rows)
        shares, d_scores = [], []
        for h in range(group_heads):
            at = slice(h * tiles, (h + 1) * tiles)
            score = jnp.where(weight > 0.0, scores[at] * scale, -1e30)
            numerator = weight * jnp.exp(score - jnp.max(score, axis=1, keepdims=True))
            share = numerator * (1.0 / jnp.sum(numerator, axis=1, keepdims=True))
            slant = share * d_share[at]
            d_score = (slant - share * jnp.sum(slant, axis=1, keepdims=True)) * scale
            shares.append(share.astype(BF))
            d_scores.append(d_score.astype(BF))
        context[:, start : start + group_width] = dot_nn(beside(shares), stacked(value_rows))
        grads["query", group] = dot_nn(beside(d_scores), stacked(key_rows))
        grads["key", group] = dot_nn(beside([part.T for part in d_scores]), query_stack)
        grads["value", group] = dot_nn(beside([part.T for part in shares]), d_out_stack)
    d_qkv[...] = beside([grads[name, group].astype(BF) for name in ("query", "key", "value") for group in range(2)])
    d_direct[...] = d_attended

    near = pl.ds(pl.multiple_of(place[1] // 4 * 16, 16), 16)
    d_slide = d_direct[near, :] + dot_nt(d_qkv[near, :], w_qkv[...])
    d_embed = dot_nt(d_slide.astype(BF), w_proj[...])
    eight = jnp.where(place[1] // 2 % 2 == 0, d_embed[:8, :], d_embed[8:, :])
    high, low = halves(eight)
    loads[3].wait()
    back = dot_nt(jnp.concatenate([high, low], axis=0), w_out[...])
    back = back[:8, :] + back[8:, :]
    back = jnp.where(core == 0, back, jnp.concatenate([back[4:, :], back[:4, :]], axis=0)) * (4.0 / tokens)
    for copy in copies:
        copy.wait()
    patches = tokens // 4
    for tile in range(8):
        at = pl.ds(tile * patches, patches)
        d_preact[at, :] = (slope[at, :].astype(F4) * back[tile : tile + 1, :]).astype(BF)


def attention(place, seg_len, gathered, weights, cot_all, slide_of, order_of, normed, slopes):
    w_proj, w_qkv, w_attn, w_out = weights
    tiles = slide_of.shape[1]
    width, slide_width = w_proj.shape
    hidden = w_out.shape[0] // 2
    tokens = slopes[0].shape[0]
    return pl.pallas_call(
        attention_kernel,
        in_specs=[SMEM, SMEM] + [VMEM] * 2 + [ANY] * 10,
        out_specs=[VMEM] * 10,
        out_shape=[
            pltpu.VMEM((2 * tokens, hidden), BF),
            *[pltpu.VMEM((width // 4, 2 * tokens), BF)] * 4,
            jax.ShapeDtypeStruct((tiles, 3 * slide_width), BF),
            jax.ShapeDtypeStruct((tiles, slide_width), F4),
            jax.ShapeDtypeStruct((tiles, slide_width), F4),
            jax.ShapeDtypeStruct((tiles, slide_width), BF),
            jax.ShapeDtypeStruct((tiles, 256), BF),
        ],
        scratch_shapes=[
            pltpu.VMEM((2 * tokens, hidden), BF),
            pltpu.VMEM(w_proj.shape, BF),
            pltpu.VMEM(w_qkv.shape, BF),
            pltpu.VMEM(w_attn.shape, BF),
            pltpu.VMEM((hidden, width), BF),
            pltpu.VMEM(gathered.shape, BF),
            pltpu.VMEM(cot_all.shape, F4),
            pltpu.SemaphoreType.DMA((40,)),
        ],
        compiler_params=pltpu.CompilerParams(vmem_limit_bytes=24 * MIB),
        name="attention",
    )(
        place,
        seg_len,
        slide_of,
        order_of,
        *[from_hbm(value) for value in (gathered, cot_all, *weights, normed[0])],
        normed[1],
        from_hbm(slopes[0]),
        slopes[1],
    )


def outputs_kernel(
    place,
    context,
    slide_rows,
    slide_of,
    counts,
    pooled_pair,
    d_qkv,
    d_direct,
    w_attn_hbm,
    w_qkv_hbm,
    w_proj_hbm,
    slide_embed,
    grad_out,
    w_attn,
    w_qkv,
    w_proj,
    sems,
):
    pairs = [(w_attn_hbm, w_attn), (w_qkv_hbm, w_qkv), (w_proj_hbm, w_proj)]
    loads = [pltpu.make_async_copy(src, dst, sems.at[i]) for i, (src, dst) in enumerate(pairs)]
    for load in loads:
        load.start()
    tiles = slide_of.shape[1]
    group = lax.broadcasted_iota(jnp.int32, (16, tiles), 0)
    member = (slide_of[...] == group).astype(F4).astype(BF)
    high, low = halves(context[...])
    loads[0].wait()
    attended = slide_rows[...].astype(F4) + dot_nn(high, w_attn[...]) + dot_nn(low, w_attn[...])
    high, low = halves(attended)
    sums = (dot_nn(member, high) + dot_nn(member, low)) / counts[...].astype(F4)
    own = sums[0:4, :]
    for index in range(1, 4):
        own = jnp.where(place[0] == index, sums[4 * index : 4 * index + 4, :], own)
    slide_embed[...] = own
    loads[1].wait()
    d_slide = d_direct[...] + dot_nt(d_qkv[...], w_qkv[...])
    loads[2].wait()
    high, low = halves(dot_nt(d_slide.astype(BF), w_proj[...]))
    pair = pooled_pair[...]
    both = dot_tn(pair, high) + dot_tn(pair, low)
    rows = grad_out.shape[0]
    grad_out[...] = both[:rows, :] + both[128 : 128 + rows, :]


def outputs(place, context, slide_rows, slide_of, counts, pooled_pair, d_qkv, d_direct, weights, rows):
    w_attn, w_qkv, w_proj = weights
    width, slide_width = w_proj.shape
    return pl.pallas_call(
        outputs_kernel,
        in_specs=[SMEM] + [VMEM] * 7 + [ANY] * 3,
        out_shape=[jax.ShapeDtypeStruct((4, slide_width), F4), jax.ShapeDtypeStruct((rows, width), F4)],
        scratch_shapes=[pltpu.VMEM(weight.shape, BF) for weight in weights] + [pltpu.SemaphoreType.DMA((3,))],
        compiler_params=pltpu.CompilerParams(vmem_limit_bytes=20 * MIB),
        cost_estimate=pl.CostEstimate(flops=1000, bytes_accessed=1000, transcendentals=0),
        name="outputs",
    )(
        place,
        context,
        slide_rows,
        slide_of,
        counts,
        pooled_pair,
        d_qkv,
        d_direct,
        *[from_hbm(weight) for weight in weights],
    )


def grad_kernel(lhs, d_preact, out):
    out[...] = dot_nn(lhs[...], d_preact[...]).astype(BF)


def grad_chunk(lhs, d_preact):
    rows, tokens = lhs.shape
    hidden = d_preact.shape[1]
    return pl.pallas_call(
        grad_kernel,
        in_specs=[VMEM] * 2,
        out_specs=VMEM,
        out_shape=jax.ShapeDtypeStruct((rows, hidden), BF),
        compiler_params=pltpu.CompilerParams(vmem_limit_bytes=16 * MIB),
        cost_estimate=pl.CostEstimate(flops=1000, bytes_accessed=1000, transcendentals=0),
        name="grad_chunk",
    )(from_vmem(lhs), from_vmem(d_preact))


def add_four_kernel(one, two, three, four, after, *outs):
    rows = outs[0].shape[0]
    for index, out in enumerate(outs):
        at = pl.ds(index * rows, rows)
        total = (one[at, :].astype(F4) + two[at, :].astype(F4)) + (three[at, :].astype(F4) + four[at, :].astype(F4))
        out[...] = total.astype(BF)


def add_four(parts, after):
    rows, columns = parts[0].shape
    return pl.pallas_call(
        add_four_kernel,
        in_specs=[VMEM] * 4 + [ANY],
        out_shape=[jax.ShapeDtypeStruct((rows // 4, columns), BF)] * 4,
        compiler_params=pltpu.CompilerParams(vmem_limit_bytes=8 * MIB),
        name="add_four",
    )(*parts, from_hbm(after))


def split_kernel(place, one, two, three, four, keep, send):
    total = (one[...].astype(F4) + two[...].astype(F4)) + (three[...].astype(F4) + four[...].astype(F4))
    rows = keep.shape[0]
    top, bottom = total[:rows, :], total[rows:, :]
    keep[...] = jnp.where(place[2] == 0, top, bottom)
    send[...] = jnp.where(place[2] == 0, bottom, top)


def split(place, parts):
    rows, columns = parts[0].shape
    return pl.pallas_call(
        split_kernel,
        in_specs=[SMEM] + [VMEM] * 4,
        out_shape=[jax.ShapeDtypeStruct((rows // 2, columns), F4)] * 2,
        compiler_params=pltpu.CompilerParams(vmem_limit_bytes=8 * MIB),
        name="split",
    )(place, *parts)


def finish_kernel(place, keep, received, out):
    half = out.shape[1] // 2
    first = place[2] == 0
    out[:, :half] = jnp.where(first, keep[...], received[...])
    out[:, half:] = jnp.where(first, received[...], keep[...])


def finish(place, keep, received):
    rows, columns = keep.shape
    return pl.pallas_call(
        finish_kernel,
        in_specs=[SMEM] + [VMEM] * 2,
        out_shape=jax.ShapeDtypeStruct((rows, 2 * columns), F4),
        compiler_params=pltpu.CompilerParams(vmem_limit_bytes=8 * MIB),
        name="finish",
    )(place, keep, received)


def moved(value, step):
    pairs = []
    for z in range(4):
        for x in range(4):
            for c in range(2):
                to_z, to_x, to_c = step(z, x, c)
                pairs.append(((z * 4 + x) * 2 + c, (to_z % 4 * 4 + to_x % 4) * 2 + to_c % 2))
    return lax.ppermute(value, "tile", pairs)


def other_core(value):
    return moved(value, lambda z, x, c: (z, x, c + 1))


def first_axis(value, k):
    return moved(value, lambda z, x, c: (z, x + k, c) if c == 0 else (z + k, x, c))


def second_axis(value, k):
    return moved(value, lambda z, x, c: (z + k, x, c) if c == 0 else (z, x + k, c))


def on_device(
    tiles,
    w_in,
    w_out,
    w_proj,
    w_qkv,
    w_attn_out,
    slide_of_tile,
    order_of_tile,
    slide_counts,
    seg_len,
    slide_cot,
):
    tile_count, patches, width = tiles.shape
    hidden = w_in.shape[1]
    peers = 32
    flat = tiles.reshape(tile_count * patches, width)
    tile_pos = lax.axis_index("tile")
    slide_pos = lax.axis_index("slide")
    place = jnp.stack([slide_pos, tile_pos, tile_pos % 2, tile_pos // 8, tile_pos // 2 % 4]).astype(jnp.int32)
    counts = slide_counts.reshape(-1, 1)
    slide_of = slide_of_tile.reshape(1, -1)
    order_of = order_of_tile.reshape(1, -1)

    slope_send, slope_keep, pooled, shared, token_mean, normed = forward(flat, w_in, w_out, slide_cot, tile_count)
    parts = [shared] + [
        lax.ppermute(shared, "slide", [(i, (i + k) % 4) for i in range(4)]) for k in (1, 2, 3)
    ]
    normed_t = transposed(normed, shared, 2 * patches)
    slices = pooled.reshape(2 * tile_count, peers, hidden // peers).transpose(1, 0, 2)
    slices = jnp.pad(slices.reshape(peers * 2 * tile_count, -1), ((0, 0), (0, 128 - hidden // peers)))
    mine, cot_all, normed_t, slope_send = embed(
        place, parts, token_mean, counts, slices, normed_t, slope_send, peers
    )
    gathered = lax.all_to_all(
        mine.reshape(peers, 8, -1), "tile", split_axis=0, concat_axis=0, tiled=True
    ).reshape(peers * 8, -1)
    slope_other, normed_other = other_core(slope_send), other_core(normed_t)
    d_preact, *lhs, d_qkv, d_direct, context, slide_rows, pooled_pair = attention(
        place,
        seg_len,
        gathered,
        (w_proj, w_qkv, w_attn_out, w_out),
        cot_all,
        slide_of,
        order_of,
        (normed_t, normed_other),
        (slope_keep, slope_other),
    )
    chunks = {}
    for k in (2, 1, 3):
        chunks[k] = first_axis(grad_chunk(lhs[k], d_preact), k)
    chunks[0] = grad_chunk(lhs[0], d_preact)
    slide_embed, grad_out = outputs(
        place,
        context,
        slide_rows,
        slide_of,
        counts,
        pooled_pair,
        d_qkv,
        d_direct,
        (w_attn_out, w_qkv, w_proj),
        hidden // peers,
    )
    parts = add_four([chunks[k] for k in range(4)], slide_embed)
    parts = [parts[0]] + [second_axis(parts[k], k) for k in (1, 2, 3)]
    keep, send = split(place, parts)
    return (slide_embed, finish(place, keep, other_core(send)), grad_out)


def solution(mesh):
    placed = (
        P("tile", None, None),
        P(None, "slide"),
        P("slide", None),
        P(),
        P(),
        P(),
        P(),
        P(),
        P(),
        P(),
        P("slide", None),
    )
    return jax.shard_map(
        on_device,
        mesh=mesh,
        in_specs=placed,
        out_specs=(P("slide", None), P("tile", "slide"), P(("slide", "tile"), None)),
        check_vma=False,
    )
```

```python
import math

import jax
import jax.numpy as jnp
from jax import lax
from jax.experimental import pallas as pl
from jax.experimental.pallas import tpu as pltpu
from jax.sharding import PartitionSpec as P

HEADS = 16
EPSILON = 1e-06
MIB = 1 << 20
BF = jnp.bfloat16
F4 = jnp.float32


def dot_nn(a, b):
    return lax.dot_general(a, b, (((1,), (0,)), ((), ())), preferred_element_type=F4)


def dot_nt(a, b):
    return lax.dot_general(a, b, (((1,), (1,)), ((), ())), preferred_element_type=F4)


def dot_tn(a, b):
    return lax.dot_general(a, b, (((0,), (0,)), ((), ())), preferred_element_type=F4)


def halves(value):
    high = value.astype(BF)
    return high, (value - high.astype(F4)).astype(BF)


def standardise(values):
    width = values.shape[1]
    centre = jnp.sum(values, axis=1, keepdims=True) * (1.0 / width)
    shifted = values - centre
    spread = jnp.sum(shifted * shifted, axis=1, keepdims=True) * (1.0 / width)
    return shifted * lax.rsqrt(spread + EPSILON)


def gelu_pair(a):
    bell = jnp.exp2(a * a * (-0.5 * 1.4426950408889634))
    t = 1.0 / (1.0 + jnp.abs(a) * (0.3275911 * 0.7071067811865476))
    series = t * (0.127414796 + t * (-0.142248368 + t * (0.7107068705 + t * (-0.7265760135 + t * 0.5307027145))))
    tail = series * bell
    phi = jnp.where(a < 0.0, tail, 1.0 - tail)
    return a * phi, phi + a * (bell * 0.3989422804014327)


def from_hbm(value):
    return pltpu.with_memory_space_constraint(value, pltpu.HBM)


def from_vmem(value):
    return pltpu.with_memory_space_constraint(value, pltpu.VMEM)


ANY = pl.BlockSpec(memory_space=pl.ANY)
SMEM = pl.BlockSpec(memory_space=pltpu.SMEM)
VMEM = pl.BlockSpec(memory_space=pltpu.VMEM)


def forward_kernel(
    tiles_hbm,
    w_in_hbm,
    w_out_hbm,
    cot_hbm,
    slope_send,
    slope_keep,
    pooled,
    shared,
    token_mean,
    normed_hbm,
    tiles,
    normed,
    w_in,
    w_out,
    slope,
    total,
    cot,
    tile_sems,
    in_sems,
    out_sems,
    normed_sems,
    slope_sems,
    cot_sem,
):
    core = lax.axis_index("tile") % 2
    tile_count = token_mean.shape[0]
    patches = tiles.shape[0] // tile_count
    steps, _, block = w_in.shape
    half = steps // 2
    pieces = [pl.ds(tile * patches, patches) for tile in range(tile_count)]

    def load_tile(tile):
        return pltpu.make_async_copy(tiles_hbm.at[pieces[tile]], tiles.at[pieces[tile]], tile_sems.at[tile])

    def columns(j):
        return pl.ds(pl.multiple_of((j + half * (1 - core)) % steps * block, block), block)

    def load_in(j):
        return pltpu.make_async_copy(w_in_hbm.at[:, columns(j)], w_in.at[j], in_sems.at[j])

    def load_out(j):
        return pltpu.make_async_copy(w_out_hbm.at[columns(j)], w_out.at[j], out_sems.at[j])

    def store_normed(tile):
        return pltpu.make_async_copy(normed.at[pieces[tile]], normed_hbm.at[pieces[tile]], normed_sems.at[tile])

    def store_slope(j, target):
        at = pl.ds(j % half * block, block)
        return pltpu.make_async_copy(slope.at[j], target.at[:, at], slope_sems.at[j])

    for tile in range(tile_count):
        load_tile(tile).start()
    load_in(0).start()
    load_cot = pltpu.make_async_copy(cot_hbm, cot, cot_sem.at[0])
    load_cot.start()
    for tile in range(tile_count):
        load_tile(tile).wait()
        if tile == 0:
            load_in(1).start()
            load_out(0).start()
        if tile == 2:
            load_in(2).start()
            load_out(1).start()
        values = tiles[pieces[tile], :].astype(F4)
        token_mean[pl.ds(tile, 1), :] = jnp.sum(values, axis=0, keepdims=True) * (1.0 / patches)
        normed[pieces[tile], :] = standardise(values).astype(BF)
        store_normed(tile).start()

    size = 128
    blocks = tiles.shape[0] // size
    per_tile = patches // size
    total[...] = jnp.zeros_like(total)

    def product(item):
        j, part = item // blocks, item % blocks
        if part == 0:
            load_in(j).wait()
            if j + 3 < steps:
                load_in(j + 3).start()
            if j + 2 < steps:
                load_out(j + 2).start()
        return dot_nn(normed[pl.ds(part * size, size), :], w_in[j])

    preact, sums = product(0), []
    for item in range(steps * blocks):
        j, part = item // blocks, item % blocks
        later = product(item + 1) if item + 1 < steps * blocks else None
        value, rate = gelu_pair(preact)
        slope[j, pl.ds(part * size, size), :] = rate.astype(BF)
        sums.append(jnp.sum(value, axis=0, keepdims=True) * (1.0 / patches))
        preact = later
        if part == blocks - 1:
            store_slope(j, slope_send if j < half else slope_keep).start()
            means = [sum(sums[i : i + per_tile]) for i in range(0, blocks, per_tile)]
            high, low = halves(jnp.concatenate(means, axis=0))
            both = jnp.concatenate([high, low], axis=0)
            pooled[:, columns(j)] = both
            load_out(j).wait()
            total[...] += dot_nn(both, w_out[j])
            sums = []
    for j in range(steps):
        store_slope(j, slope_send if j < half else slope_keep).wait()
    width = total.shape[1]
    shared[:, :width] = total[:tile_count, :] + total[tile_count:, :]
    load_cot.wait()
    shared[:, width:] = cot[...]
    for tile in range(tile_count):
        store_normed(tile).wait()


def forward(tiles, w_in, w_out, cot, tile_count):
    tokens, width = tiles.shape
    hidden = w_in.shape[1]
    block = 256
    steps = hidden // block
    slide_width = cot.shape[1]
    return pl.pallas_call(
        forward_kernel,
        in_specs=[ANY] * 4,
        out_specs=[ANY, ANY, VMEM, VMEM, VMEM, ANY],
        out_shape=[
            pltpu.HBM((tokens, hidden // 2), BF),
            pltpu.HBM((tokens, hidden // 2), BF),
            jax.ShapeDtypeStruct((2 * tile_count, hidden), BF),
            jax.ShapeDtypeStruct((tile_count, width + slide_width), F4),
            jax.ShapeDtypeStruct((tile_count, width), F4),
            pltpu.HBM((tokens, width), BF),
        ],
        scratch_shapes=[
            pltpu.VMEM((tokens, width), BF),
            pltpu.VMEM((tokens, width), BF),
            pltpu.VMEM((steps, width, block), BF),
            pltpu.VMEM((steps, block, width), BF),
            pltpu.VMEM((steps, tokens, block), BF),
            pltpu.VMEM((2 * tile_count, width), F4),
            pltpu.VMEM(cot.shape, F4),
            pltpu.SemaphoreType.DMA((tile_count,)),
            pltpu.SemaphoreType.DMA((steps,)),
            pltpu.SemaphoreType.DMA((steps,)),
            pltpu.SemaphoreType.DMA((tile_count,)),
            pltpu.SemaphoreType.DMA((steps,)),
            pltpu.SemaphoreType.DMA((1,)),
        ],
        compiler_params=pltpu.CompilerParams(vmem_limit_bytes=40 * MIB),
        name="forward",
    )(from_hbm(tiles), from_hbm(w_in), from_hbm(w_out), from_hbm(cot))


def transpose_kernel(after, normed, out):
    out[...] = normed[...].T


def transposed(normed, after, patches):
    tokens, width = normed.shape
    return pl.pallas_call(
        transpose_kernel,
        grid=(tokens // patches,),
        in_specs=[ANY, pl.BlockSpec((patches, width), lambda i: (i, 0))],
        out_specs=pl.BlockSpec((width, patches), lambda i: (0, i)),
        out_shape=pltpu.HBM((width, tokens), BF),
        compiler_params=pltpu.CompilerParams(vmem_limit_bytes=16 * MIB),
        cost_estimate=pl.CostEstimate(flops=20_000_000, bytes_accessed=9_000_000, transcendentals=0),
        name="transposed",
    )(after, from_hbm(normed))


def embed_kernel(
    place, own, one, two, three, token_mean, counts, pooled, normed_in, slope_in, out, cot_all, normed_out, slope_out
):
    width = token_mean.shape[1]
    half = width // 2
    total = (own[:, :width] + two[:, :width]) + (one[:, :width] + three[:, :width])
    embedding = total + token_mean[...]
    eight = jnp.concatenate([embedding[:, :half], embedding[:, half:]], axis=0)
    out[:, :half] = jnp.concatenate([eight] * (out.shape[0] // 8), axis=0).astype(BF)
    out[:, half:] = pooled[...]
    parts = [own[:, width:], one[:, width:], two[:, width:], three[:, width:]]
    blocks = []
    for group in range(4):
        back = jnp.bitwise_and(place[0] - group, 3)
        block = parts[0]
        for shift in range(1, 4):
            block = jnp.where(back == shift, parts[shift], block)
        blocks.append(block)
    cot_all[...] = jnp.concatenate(blocks, axis=0) / counts[...].astype(F4)


def embed(place, parts, token_mean, counts, pooled, normed, slope, peers):
    tile_count, width = token_mean.shape
    slide_width = parts[0].shape[1] - width
    return pl.pallas_call(
        embed_kernel,
        in_specs=[SMEM] + [VMEM] * 7 + [ANY] * 2,
        out_specs=[VMEM] * 2 + [ANY] * 2,
        out_shape=[
            jax.ShapeDtypeStruct((peers * 8, width // 2 + 128), BF),
            jax.ShapeDtypeStruct((16, slide_width), F4),
            pltpu.HBM(normed.shape, BF),
            pltpu.HBM(slope.shape, BF),
        ],
        input_output_aliases={8: 2, 9: 3},
        compiler_params=pltpu.CompilerParams(vmem_limit_bytes=8 * MIB),
        name="embed",
    )(place, *parts, token_mean, counts, pooled, from_hbm(normed), from_hbm(slope))


def attention_kernel(
    place,
    seg_len,
    slide_of,
    order_of,
    gathered_hbm,
    cot_hbm,
    w_proj_hbm,
    w_qkv_hbm,
    w_attn_hbm,
    w_out_hbm,
    normed_own,
    normed_other,
    slope_own,
    slope_other,
    d_preact,
    lhs0,
    lhs1,
    lhs2,
    lhs3,
    d_qkv,
    d_direct,
    context,
    slide_rows,
    pooled_pair,
    slope,
    w_proj,
    w_qkv,
    w_attn,
    w_out,
    gathered,
    cot_all,
    sems,
):
    hidden = w_out.shape[0]
    half_rows = pl.ds(pl.multiple_of(place[2] * hidden, hidden), hidden)
    pairs = [(w_proj_hbm, w_proj), (w_qkv_hbm, w_qkv), (w_attn_hbm, w_attn), (w_out_hbm.at[half_rows], w_out)]
    pairs += [(gathered_hbm, gathered), (cot_hbm, cot_all)]
    loads = [pltpu.make_async_copy(src, dst, sems.at[34 + i]) for i, (src, dst) in enumerate(pairs)]
    for index in (4, 0, 5, 2, 1):
        loads[index].start()

    tokens = slope_own.shape[0]
    rows_each = lhs0.shape[0] // 4
    core = place[2]
    copies = [
        pltpu.make_async_copy(slope_own, slope.at[pl.ds(0, tokens)], sems.at[0]),
        pltpu.make_async_copy(slope_other, slope.at[pl.ds(tokens, tokens)], sems.at[1]),
    ]
    for chunk, lhs in enumerate((lhs0, lhs1, lhs2, lhs3)):
        for sub in range(4):
            z = (place[3] + jnp.where(core == 0, sub, chunk)) % 4
            x = (place[4] + jnp.where(core == 0, chunk, sub)) % 4
            source = pl.ds(pl.multiple_of((z * 4 + x) * rows_each, 16), rows_each)
            rows = pl.ds(sub * rows_each, rows_each)
            at = 2 + 2 * (4 * chunk + sub)
            copies.append(pltpu.make_async_copy(normed_own.at[source], lhs.at[rows, pl.ds(0, tokens)], sems.at[at]))
            copies.append(
                pltpu.make_async_copy(normed_other.at[source], lhs.at[rows, pl.ds(tokens, tokens)], sems.at[at + 1])
            )
    tiles = slide_of.shape[1]
    half = w_proj.shape[0] // 2
    width = w_proj.shape[1]
    head = width // HEADS

    slide = slide_of[...].astype(F4)
    order = order_of[...].astype(F4)
    weight = jnp.zeros((tiles, tiles), F4)
    for branch in range(3):
        length = seg_len[branch].astype(F4)
        block = jnp.floor((order + 0.5) / length)
        dilation = float(2**branch)
        phase = order - dilation * jnp.floor(order * (1.0 / dilation))
        code = jnp.broadcast_to((slide * 64.0 + block) * 4.0 + phase, (tiles, tiles))
        weight = weight + (code == code.T).astype(F4)
    slide_col = jnp.broadcast_to(slide, (tiles, tiles)).T
    lane = lax.broadcasted_iota(jnp.int32, (tiles, 16), 1).astype(F4)
    member = (slide_col[:, :16] == lane).astype(F4).astype(BF)
    row = lax.broadcasted_iota(jnp.int32, (tiles, 2 * tiles), 0)
    col = lax.broadcasted_iota(jnp.int32, (tiles, 2 * tiles), 1)
    first = (row // 4) * 8 + row % 4
    loads[4].wait()
    every = gathered[...]
    left = dot_nn((col == first).astype(F4).astype(BF), every).astype(BF)
    right = dot_nn((col == first + 4).astype(F4).astype(BF), every).astype(BF)
    pooled_pair[:, :128] = left[:, half:]
    pooled_pair[:, 128:] = right[:, half:]
    loads[0].wait()
    rows = (dot_nn(left[:, :half], w_proj[:half, :]) + dot_nn(right[:, :half], w_proj[half:, :])).astype(BF)
    slide_rows[...] = rows
    loads[5].wait()
    cot_high, cot_low = halves(cot_all[...])
    d_attended = dot_nn(member, cot_high) + dot_nn(member, cot_low)
    loads[2].wait()
    d_context = dot_nt(d_attended.astype(BF), w_attn[...]).astype(BF)
    loads[1].wait()
    loads[3].start()
    for copy in copies:
        copy.start()
    qkv = dot_nn(rows, w_qkv[...]).astype(BF)

    scale = 1.0 / math.sqrt(head)
    group_heads = HEADS // 2
    group_width = group_heads * head
    lanes = lax.broadcasted_iota(jnp.int32, (1, group_width), 1)
    masks = [((lanes >= h * head) & (lanes < (h + 1) * head)).astype(F4).astype(BF) for h in range(group_heads)]

    def stacked(value):
        return jnp.concatenate([value * mask for mask in masks], axis=0)

    def beside(parts):
        return jnp.concatenate(parts, axis=1)

    grads = {}
    for group in range(2):
        start = group * group_width
        query = qkv[:, start : start + group_width]
        key_rows = qkv[:, width + start : width + start + group_width]
        value_rows = qkv[:, 2 * width + start : 2 * width + start + group_width]
        d_out = d_context[:, start : start + group_width]
        query_stack, d_out_stack = stacked(query), stacked(d_out)
        scores = dot_nt(query_stack, key_rows)
        d_share = dot_nt(d_out_stack, value_rows)
        shares, d_scores = [], []
        for h in range(group_heads):
            at = slice(h * tiles, (h + 1) * tiles)
            score = jnp.where(weight > 0.0, scores[at] * scale, -1e30)
            numerator = weight * jnp.exp(score - jnp.max(score, axis=1, keepdims=True))
            share = numerator * (1.0 / jnp.sum(numerator, axis=1, keepdims=True))
            slant = share * d_share[at]
            d_score = (slant - share * jnp.sum(slant, axis=1, keepdims=True)) * scale
            shares.append(share.astype(BF))
            d_scores.append(d_score.astype(BF))
        context[:, start : start + group_width] = dot_nn(beside(shares), stacked(value_rows))
        grads["query", group] = dot_nn(beside(d_scores), stacked(key_rows))
        grads["key", group] = dot_nn(beside([part.T for part in d_scores]), query_stack)
        grads["value", group] = dot_nn(beside([part.T for part in shares]), d_out_stack)
    d_qkv[...] = beside([grads[name, group].astype(BF) for name in ("query", "key", "value") for group in range(2)])
    d_direct[...] = d_attended

    near = pl.ds(pl.multiple_of(place[1] // 4 * 16, 16), 16)
    d_slide = d_direct[near, :] + dot_nt(d_qkv[near, :], w_qkv[...])
    d_embed = dot_nt(d_slide.astype(BF), w_proj[...])
    eight = jnp.where(place[1] // 2 % 2 == 0, d_embed[:8, :], d_embed[8:, :])
    high, low = halves(eight)
    loads[3].wait()
    back = dot_nt(jnp.concatenate([high, low], axis=0), w_out[...])
    back = back[:8, :] + back[8:, :]
    back = jnp.where(core == 0, back, jnp.concatenate([back[4:, :], back[:4, :]], axis=0)) * (4.0 / tokens)
    for copy in copies:
        copy.wait()
    patches = tokens // 4
    for tile in range(8):
        at = pl.ds(tile * patches, patches)
        d_preact[at, :] = (slope[at, :].astype(F4) * back[tile : tile + 1, :]).astype(BF)


def attention(place, seg_len, gathered, weights, cot_all, slide_of, order_of, normed, slopes):
    w_proj, w_qkv, w_attn, w_out = weights
    tiles = slide_of.shape[1]
    width, slide_width = w_proj.shape
    hidden = w_out.shape[0] // 2
    tokens = slopes[0].shape[0]
    return pl.pallas_call(
        attention_kernel,
        in_specs=[SMEM, SMEM] + [VMEM] * 2 + [ANY] * 10,
        out_specs=[VMEM] * 10,
        out_shape=[
            pltpu.VMEM((2 * tokens, hidden), BF),
            *[pltpu.VMEM((width // 4, 2 * tokens), BF)] * 4,
            jax.ShapeDtypeStruct((tiles, 3 * slide_width), BF),
            jax.ShapeDtypeStruct((tiles, slide_width), F4),
            jax.ShapeDtypeStruct((tiles, slide_width), F4),
            jax.ShapeDtypeStruct((tiles, slide_width), BF),
            jax.ShapeDtypeStruct((tiles, 256), BF),
        ],
        scratch_shapes=[
            pltpu.VMEM((2 * tokens, hidden), BF),
            pltpu.VMEM(w_proj.shape, BF),
            pltpu.VMEM(w_qkv.shape, BF),
            pltpu.VMEM(w_attn.shape, BF),
            pltpu.VMEM((hidden, width), BF),
            pltpu.VMEM(gathered.shape, BF),
            pltpu.VMEM(cot_all.shape, F4),
            pltpu.SemaphoreType.DMA((40,)),
        ],
        compiler_params=pltpu.CompilerParams(vmem_limit_bytes=24 * MIB),
        name="attention",
    )(
        place,
        seg_len,
        slide_of,
        order_of,
        *[from_hbm(value) for value in (gathered, cot_all, *weights, normed[0])],
        normed[1],
        from_hbm(slopes[0]),
        slopes[1],
    )


def embed_out_kernel(place, context, slide_rows, slide_of, counts, w_attn, slide_embed):
    tiles = slide_of.shape[1]
    group = lax.broadcasted_iota(jnp.int32, (16, tiles), 0)
    member = (slide_of[...] == group).astype(F4).astype(BF)
    high, low = halves(context[...])
    attended = slide_rows[...].astype(F4) + dot_nn(high, w_attn[...]) + dot_nn(low, w_attn[...])
    high, low = halves(attended)
    sums = (dot_nn(member, high) + dot_nn(member, low)) / counts[...].astype(F4)
    own = sums[0:4, :]
    for index in range(1, 4):
        own = jnp.where(place[0] == index, sums[4 * index : 4 * index + 4, :], own)
    slide_embed[...] = own


def embed_out(place, context, slide_rows, slide_of, counts, w_attn):
    return pl.pallas_call(
        embed_out_kernel,
        in_specs=[SMEM] + [VMEM] * 5,
        out_shape=jax.ShapeDtypeStruct((4, w_attn.shape[0]), F4),
        compiler_params=pltpu.CompilerParams(vmem_limit_bytes=12 * MIB),
        cost_estimate=pl.CostEstimate(flops=1000, bytes_accessed=1000, transcendentals=0),
        name="embed_out",
    )(place, context, slide_rows, slide_of, counts, w_attn)


def grad_out_kernel(pooled_pair, d_qkv, d_direct, w_qkv_hbm, w_proj_hbm, grad_out, w_qkv, w_proj, sems):
    pairs = [(w_qkv_hbm, w_qkv), (w_proj_hbm, w_proj)]
    loads = [pltpu.make_async_copy(src, dst, sems.at[i]) for i, (src, dst) in enumerate(pairs)]
    for load in loads:
        load.start()
    loads[0].wait()
    d_slide = d_direct[...] + dot_nt(d_qkv[...], w_qkv[...])
    loads[1].wait()
    high, low = halves(dot_nt(d_slide.astype(BF), w_proj[...]))
    pair = pooled_pair[...]
    both = dot_tn(pair, high) + dot_tn(pair, low)
    rows = grad_out.shape[0]
    grad_out[...] = both[:rows, :] + both[128 : 128 + rows, :]


def grad_out_of(pooled_pair, d_qkv, d_direct, weights, rows):
    return pl.pallas_call(
        grad_out_kernel,
        in_specs=[VMEM] * 3 + [ANY] * 2,
        out_shape=jax.ShapeDtypeStruct((rows, weights[1].shape[0]), F4),
        scratch_shapes=[pltpu.VMEM(weight.shape, BF) for weight in weights] + [pltpu.SemaphoreType.DMA((2,))],
        compiler_params=pltpu.CompilerParams(vmem_limit_bytes=20 * MIB),
        cost_estimate=pl.CostEstimate(flops=1000, bytes_accessed=1000, transcendentals=0),
        name="grad_out",
    )(pooled_pair, d_qkv, d_direct, *[from_hbm(weight) for weight in weights])


def grad_kernel(lhs, d_preact, *outs):
    rows = outs[0].shape[0]
    for index, out in enumerate(outs):
        out[...] = dot_nn(lhs[index * rows : (index + 1) * rows, :], d_preact[...]).astype(BF)


def grad_chunk(lhs, d_preact, parts=1):
    rows = lhs.shape[0]
    hidden = d_preact.shape[1]
    return pl.pallas_call(
        grad_kernel,
        in_specs=[VMEM] * 2,
        out_specs=[VMEM] * parts,
        out_shape=[jax.ShapeDtypeStruct((rows // parts, hidden), BF)] * parts,
        compiler_params=pltpu.CompilerParams(vmem_limit_bytes=16 * MIB),
        cost_estimate=pl.CostEstimate(flops=1000, bytes_accessed=1000, transcendentals=0),
        name="grad_chunk",
    )(from_vmem(lhs), from_vmem(d_preact))


def relay_kernel(up, down, up_received, down_received, after, up_out, down_out):
    half = up_received.shape[0]
    up_out[:half, :] = (up[:half, :].astype(F4) + up_received[...].astype(F4)).astype(BF)
    up_out[half:, :] = up[half:, :]
    down_out[:half, :] = down[:half, :]
    down_out[half:, :] = (down[half:, :].astype(F4) + down_received[...].astype(F4)).astype(BF)


def relay(up, down, up_received, down_received, after):
    return pl.pallas_call(
        relay_kernel,
        in_specs=[VMEM] * 4 + [ANY],
        out_shape=[jax.ShapeDtypeStruct(up.shape, BF)] * 2,
        compiler_params=pltpu.CompilerParams(vmem_limit_bytes=8 * MIB),
        name="relay",
    )(up, down, up_received, down_received, after)


def add_three_kernel(one, two, three, after, *outs):
    rows = outs[0].shape[0]
    for index, out in enumerate(outs):
        at = pl.ds(index * rows, rows)
        out[...] = (one[at, :].astype(F4) + two[at, :].astype(F4) + three[at, :].astype(F4)).astype(BF)


def add_three(parts, after):
    rows, columns = parts[0].shape
    return pl.pallas_call(
        add_three_kernel,
        in_specs=[VMEM] * 3 + [ANY],
        out_shape=[jax.ShapeDtypeStruct((rows // 4, columns), BF)] * 4,
        compiler_params=pltpu.CompilerParams(vmem_limit_bytes=8 * MIB),
        name="add_three",
    )(*parts, from_hbm(after))


def split_kernel(place, one, two, three, four, after, keep, send):
    total = (one[...].astype(F4) + two[...].astype(F4)) + (three[...].astype(F4) + four[...].astype(F4))
    rows = keep.shape[0]
    top, bottom = total[:rows, :], total[rows:, :]
    keep[...] = jnp.where(place[2] == 0, top, bottom)
    send[...] = jnp.where(place[2] == 0, bottom, top)


def split(place, parts, after):
    rows, columns = parts[0].shape
    return pl.pallas_call(
        split_kernel,
        in_specs=[SMEM] + [VMEM] * 4 + [ANY],
        out_shape=[jax.ShapeDtypeStruct((rows // 2, columns), F4)] * 2,
        compiler_params=pltpu.CompilerParams(vmem_limit_bytes=8 * MIB),
        name="split",
    )(place, *parts, from_hbm(after))


def finish_kernel(place, keep, received, out):
    half = out.shape[1] // 2
    first = place[2] == 0
    out[:, :half] = jnp.where(first, keep[...], received[...])
    out[:, half:] = jnp.where(first, received[...], keep[...])


def finish(place, keep, received):
    rows, columns = keep.shape
    return pl.pallas_call(
        finish_kernel,
        in_specs=[SMEM] + [VMEM] * 2,
        out_shape=jax.ShapeDtypeStruct((rows, 2 * columns), F4),
        compiler_params=pltpu.CompilerParams(vmem_limit_bytes=8 * MIB),
        name="finish",
    )(place, keep, received)


def moved(value, step):
    pairs = []
    for z in range(4):
        for x in range(4):
            for c in range(2):
                to_z, to_x, to_c = step(z, x, c)
                pairs.append(((z * 4 + x) * 2 + c, (to_z % 4 * 4 + to_x % 4) * 2 + to_c % 2))
    return lax.ppermute(value, "tile", pairs)


def other_core(value):
    return moved(value, lambda z, x, c: (z, x, c + 1))


def first_axis(value, k):
    return moved(value, lambda z, x, c: (z, x + k, c) if c == 0 else (z + k, x, c))


def second_axis(value, k):
    return moved(value, lambda z, x, c: (z + k, x, c) if c == 0 else (z, x + k, c))


def on_device(
    tiles,
    w_in,
    w_out,
    w_proj,
    w_qkv,
    w_attn_out,
    slide_of_tile,
    order_of_tile,
    slide_counts,
    seg_len,
    slide_cot,
):
    tile_count, patches, width = tiles.shape
    hidden = w_in.shape[1]
    peers = 32
    flat = tiles.reshape(tile_count * patches, width)
    tile_pos = lax.axis_index("tile")
    slide_pos = lax.axis_index("slide")
    place = jnp.stack([slide_pos, tile_pos, tile_pos % 2, tile_pos // 8, tile_pos // 2 % 4]).astype(jnp.int32)
    counts = slide_counts.reshape(-1, 1)
    slide_of = slide_of_tile.reshape(1, -1)
    order_of = order_of_tile.reshape(1, -1)

    slope_send, slope_keep, pooled, shared, token_mean, normed = forward(flat, w_in, w_out, slide_cot, tile_count)
    parts = [shared] + [
        lax.ppermute(shared, "slide", [(i, (i + k) % 4) for i in range(4)]) for k in (1, 2, 3)
    ]
    normed_t = transposed(normed, shared, 2 * patches)
    slices = pooled.reshape(2 * tile_count, peers, hidden // peers).transpose(1, 0, 2)
    slices = jnp.pad(slices.reshape(peers * 2 * tile_count, -1), ((0, 0), (0, 128 - hidden // peers)))
    mine, cot_all, normed_t, slope_send = embed(
        place, parts, token_mean, counts, slices, normed_t, slope_send, peers
    )
    gathered = lax.all_to_all(
        mine.reshape(peers, 8, -1), "tile", split_axis=0, concat_axis=0, tiled=True
    ).reshape(peers * 8, -1)
    slope_other, normed_other = other_core(slope_send), other_core(normed_t)
    d_preact, *lhs, d_qkv, d_direct, context, slide_rows, pooled_pair = attention(
        place,
        seg_len,
        gathered,
        (w_proj, w_qkv, w_attn_out, w_out),
        cot_all,
        slide_of,
        order_of,
        (normed_t, normed_other),
        (slope_keep, slope_other),
    )
    upper, lower = grad_chunk(lhs[2], d_preact, 2)
    up_received, down_received = first_axis(upper, 1), first_axis(lower, 3)
    up, down = grad_chunk(lhs[1], d_preact)[0], grad_chunk(lhs[3], d_preact)[0]
    own = grad_chunk(lhs[0], d_preact)[0]
    up, down = relay(up, down, up_received, down_received, own)
    parts = [own, first_axis(up, 1), first_axis(down, 3)]
    grad_out = grad_out_of(pooled_pair, d_qkv, d_direct, (w_qkv, w_proj), hidden // peers)
    slide_embed = embed_out(place, context, slide_rows, slide_of, counts, w_attn_out)
    parts = add_three(parts, grad_out)
    parts = [parts[0]] + [second_axis(parts[k], k) for k in (1, 2, 3)]
    keep, send = split(place, parts, slide_embed)
    return (slide_embed, finish(place, keep, other_core(send)), grad_out)


def solution(mesh):
    placed = (
        P("tile", None, None),
        P(None, "slide"),
        P("slide", None),
        P(),
        P(),
        P(),
        P(),
        P(),
        P(),
        P(),
        P("slide", None),
    )
    return jax.shard_map(
        on_device,
        mesh=mesh,
        in_specs=placed,
        out_specs=(P("slide", None), P("tile", "slide"), P(("slide", "tile"), None)),
        check_vma=False,
    )
```

```python
import math

import jax
import jax.numpy as jnp
from jax import lax
from jax.experimental import pallas as pl
from jax.experimental.pallas import tpu as pltpu
from jax.sharding import PartitionSpec as P

HEADS = 16
EPSILON = 1e-06
MIB = 1 << 20
BF = jnp.bfloat16
F4 = jnp.float32


def dot_nn(a, b):
    return lax.dot_general(a, b, (((1,), (0,)), ((), ())), preferred_element_type=F4)


def dot_nt(a, b):
    return lax.dot_general(a, b, (((1,), (1,)), ((), ())), preferred_element_type=F4)


def dot_tn(a, b):
    return lax.dot_general(a, b, (((0,), (0,)), ((), ())), preferred_element_type=F4)


def halves(value):
    high = value.astype(BF)
    return high, (value - high.astype(F4)).astype(BF)


def standardise(values):
    width = values.shape[1]
    centre = jnp.sum(values, axis=1, keepdims=True) * (1.0 / width)
    shifted = values - centre
    spread = jnp.sum(shifted * shifted, axis=1, keepdims=True) * (1.0 / width)
    return shifted * lax.rsqrt(spread + EPSILON)


def gelu_pair(a):
    bell = jnp.exp2(a * a * (-0.5 * 1.4426950408889634))
    t = 1.0 / (1.0 + jnp.abs(a) * (0.3275911 * 0.7071067811865476))
    series = t * (0.127414796 + t * (-0.142248368 + t * (0.7107068705 + t * (-0.7265760135 + t * 0.5307027145))))
    tail = series * bell
    phi = jnp.where(a < 0.0, tail, 1.0 - tail)
    return a * phi, phi + a * (bell * 0.3989422804014327)


def from_hbm(value):
    return pltpu.with_memory_space_constraint(value, pltpu.HBM)


def from_vmem(value):
    return pltpu.with_memory_space_constraint(value, pltpu.VMEM)


ANY = pl.BlockSpec(memory_space=pl.ANY)
SMEM = pl.BlockSpec(memory_space=pltpu.SMEM)
VMEM = pl.BlockSpec(memory_space=pltpu.VMEM)


def forward_kernel(
    tiles_hbm,
    w_in_hbm,
    w_out_hbm,
    cot_hbm,
    slope_send,
    slope_keep,
    pooled,
    shared,
    token_mean,
    normed_hbm,
    tiles,
    normed,
    w_in,
    w_out,
    slope,
    total,
    cot,
    tile_sems,
    in_sems,
    out_sems,
    normed_sems,
    slope_sems,
    cot_sem,
):
    core = lax.axis_index("tile") % 2
    tile_count = token_mean.shape[0]
    patches = tiles.shape[0] // tile_count
    steps, _, block = w_in.shape
    half = steps // 2
    pieces = [pl.ds(tile * patches, patches) for tile in range(tile_count)]

    def load_tile(tile):
        return pltpu.make_async_copy(tiles_hbm.at[pieces[tile]], tiles.at[pieces[tile]], tile_sems.at[tile])

    def columns(j):
        return pl.ds(pl.multiple_of((j + half * (1 - core)) % steps * block, block), block)

    def load_in(j):
        return pltpu.make_async_copy(w_in_hbm.at[:, columns(j)], w_in.at[j], in_sems.at[j])

    def load_out(j):
        return pltpu.make_async_copy(w_out_hbm.at[columns(j)], w_out.at[j], out_sems.at[j])

    def store_normed(tile):
        return pltpu.make_async_copy(normed.at[pieces[tile]], normed_hbm.at[pieces[tile]], normed_sems.at[tile])

    def store_slope(j, target):
        at = pl.ds(j % half * block, block)
        return pltpu.make_async_copy(slope.at[j], target.at[:, at], slope_sems.at[j])

    for tile in range(tile_count):
        load_tile(tile).start()
    load_in(0).start()
    load_cot = pltpu.make_async_copy(cot_hbm, cot, cot_sem.at[0])
    load_cot.start()
    for tile in range(tile_count):
        load_tile(tile).wait()
        if tile == 0:
            load_in(1).start()
            load_out(0).start()
        if tile == 2:
            load_in(2).start()
            load_out(1).start()
        values = tiles[pieces[tile], :].astype(F4)
        token_mean[pl.ds(tile, 1), :] = jnp.sum(values, axis=0, keepdims=True) * (1.0 / patches)
        normed[pieces[tile], :] = standardise(values).astype(BF)
        store_normed(tile).start()

    size = 128
    blocks = tiles.shape[0] // size
    per_tile = patches // size

    def product(item):
        j, part = item // blocks, item % blocks
        if part == 0:
            load_in(j).wait()
            if j + 3 < steps:
                load_in(j + 3).start()
            if j + 2 < steps:
                load_out(j + 2).start()
        return dot_nn(normed[pl.ds(part * size, size), :], w_in[j])

    preact, sums, boths = product(0), [], []
    for item in range(steps * blocks):
        j, part = item // blocks, item % blocks
        later = product(item + 1) if item + 1 < steps * blocks else None
        value, rate = gelu_pair(preact)
        slope[j, pl.ds(part * size, size), :] = rate.astype(BF)
        sums.append(jnp.sum(value, axis=0, keepdims=True) * (1.0 / patches))
        preact = later
        if part == blocks - 1:
            store_slope(j, slope_send if j < half else slope_keep).start()
            means = [sum(sums[i : i + per_tile]) for i in range(0, blocks, per_tile)]
            high, low = halves(jnp.concatenate(means, axis=0))
            both = jnp.concatenate([high, low], axis=0)
            pooled[:, columns(j)] = both
            boths.append(both)
            sums = []
    for j in range(steps):
        store_slope(j, slope_send if j < half else slope_keep).wait()
    for j in range(steps):
        load_out(j).wait()
    total[...] = dot_nn(jnp.concatenate(boths, axis=1), w_out[...].reshape(-1, w_out.shape[2]))
    width = total.shape[1]
    shared[:, :width] = total[:tile_count, :] + total[tile_count:, :]
    load_cot.wait()
    shared[:, width:] = cot[...]
    for tile in range(tile_count):
        store_normed(tile).wait()


def forward(tiles, w_in, w_out, cot, tile_count):
    tokens, width = tiles.shape
    hidden = w_in.shape[1]
    block = 256
    steps = hidden // block
    slide_width = cot.shape[1]
    return pl.pallas_call(
        forward_kernel,
        in_specs=[ANY] * 4,
        out_specs=[ANY, ANY, VMEM, VMEM, VMEM, ANY],
        out_shape=[
            pltpu.HBM((tokens, hidden // 2), BF),
            pltpu.HBM((tokens, hidden // 2), BF),
            jax.ShapeDtypeStruct((2 * tile_count, hidden), BF),
            jax.ShapeDtypeStruct((tile_count, width + slide_width), F4),
            jax.ShapeDtypeStruct((tile_count, width), F4),
            pltpu.HBM((tokens, width), BF),
        ],
        scratch_shapes=[
            pltpu.VMEM((tokens, width), BF),
            pltpu.VMEM((tokens, width), BF),
            pltpu.VMEM((steps, width, block), BF),
            pltpu.VMEM((steps, block, width), BF),
            pltpu.VMEM((steps, tokens, block), BF),
            pltpu.VMEM((2 * tile_count, width), F4),
            pltpu.VMEM(cot.shape, F4),
            pltpu.SemaphoreType.DMA((tile_count,)),
            pltpu.SemaphoreType.DMA((steps,)),
            pltpu.SemaphoreType.DMA((steps,)),
            pltpu.SemaphoreType.DMA((tile_count,)),
            pltpu.SemaphoreType.DMA((steps,)),
            pltpu.SemaphoreType.DMA((1,)),
        ],
        compiler_params=pltpu.CompilerParams(vmem_limit_bytes=40 * MIB),
        name="forward",
    )(from_hbm(tiles), from_hbm(w_in), from_hbm(w_out), from_hbm(cot))


def transpose_kernel(after, normed, out):
    out[...] = normed[...].T


def transposed(normed, after, patches):
    tokens, width = normed.shape
    return pl.pallas_call(
        transpose_kernel,
        grid=(tokens // patches,),
        in_specs=[ANY, pl.BlockSpec((patches, width), lambda i: (i, 0))],
        out_specs=pl.BlockSpec((width, patches), lambda i: (0, i)),
        out_shape=pltpu.HBM((width, tokens), BF),
        compiler_params=pltpu.CompilerParams(vmem_limit_bytes=16 * MIB),
        cost_estimate=pl.CostEstimate(flops=20_000_000, bytes_accessed=9_000_000, transcendentals=0),
        name="transposed",
    )(after, from_hbm(normed))


def embed_kernel(
    place, own, one, two, three, token_mean, counts, pooled, normed_in, slope_in, out, cot_all, normed_out, slope_out
):
    width = token_mean.shape[1]
    half = width // 2
    total = (own[:, :width] + two[:, :width]) + (one[:, :width] + three[:, :width])
    embedding = total + token_mean[...]
    eight = jnp.concatenate([embedding[:, :half], embedding[:, half:]], axis=0)
    out[:, :half] = jnp.concatenate([eight] * (out.shape[0] // 8), axis=0).astype(BF)
    out[:, half:] = pooled[...]
    parts = [own[:, width:], one[:, width:], two[:, width:], three[:, width:]]
    blocks = []
    for group in range(4):
        back = jnp.bitwise_and(place[0] - group, 3)
        block = parts[0]
        for shift in range(1, 4):
            block = jnp.where(back == shift, parts[shift], block)
        blocks.append(block)
    cot_all[...] = jnp.concatenate(blocks, axis=0) / counts[...].astype(F4)


def embed(place, parts, token_mean, counts, pooled, normed, slope, peers):
    tile_count, width = token_mean.shape
    slide_width = parts[0].shape[1] - width
    return pl.pallas_call(
        embed_kernel,
        in_specs=[SMEM] + [VMEM] * 7 + [ANY] * 2,
        out_specs=[VMEM] * 2 + [ANY] * 2,
        out_shape=[
            jax.ShapeDtypeStruct((peers * 8, width // 2 + 128), BF),
            jax.ShapeDtypeStruct((16, slide_width), F4),
            pltpu.HBM(normed.shape, BF),
            pltpu.HBM(slope.shape, BF),
        ],
        input_output_aliases={8: 2, 9: 3},
        compiler_params=pltpu.CompilerParams(vmem_limit_bytes=8 * MIB),
        name="embed",
    )(place, *parts, token_mean, counts, pooled, from_hbm(normed), from_hbm(slope))


def attention_kernel(
    place,
    seg_len,
    slide_of,
    order_of,
    gathered_hbm,
    cot_hbm,
    w_proj_hbm,
    w_qkv_hbm,
    w_attn_hbm,
    w_out_hbm,
    normed_own,
    normed_other,
    slope_own,
    slope_other,
    d_preact,
    lhs0,
    lhs1,
    lhs3,
    upper,
    lower,
    d_qkv,
    d_direct,
    context,
    slide_rows,
    pooled_pair,
    lhs2,
    slope,
    w_proj,
    w_qkv,
    w_attn,
    w_out,
    gathered,
    cot_all,
    sems,
):
    hidden = w_out.shape[0]
    half_rows = pl.ds(pl.multiple_of(place[2] * hidden, hidden), hidden)
    pairs = [(w_proj_hbm, w_proj), (w_qkv_hbm, w_qkv), (w_attn_hbm, w_attn), (w_out_hbm.at[half_rows], w_out)]
    pairs += [(gathered_hbm, gathered), (cot_hbm, cot_all)]
    loads = [pltpu.make_async_copy(src, dst, sems.at[34 + i]) for i, (src, dst) in enumerate(pairs)]
    for index in (4, 0, 5, 2, 1):
        loads[index].start()

    tokens = slope_own.shape[0]
    rows_each = lhs0.shape[0] // 4
    core = place[2]
    copies = [
        pltpu.make_async_copy(slope_own, slope.at[pl.ds(0, tokens)], sems.at[0]),
        pltpu.make_async_copy(slope_other, slope.at[pl.ds(tokens, tokens)], sems.at[1]),
    ]
    for chunk, lhs in enumerate((lhs0, lhs1, lhs2, lhs3)):
        for sub in range(4):
            z = (place[3] + jnp.where(core == 0, sub, chunk)) % 4
            x = (place[4] + jnp.where(core == 0, chunk, sub)) % 4
            source = pl.ds(pl.multiple_of((z * 4 + x) * rows_each, 16), rows_each)
            rows = pl.ds(sub * rows_each, rows_each)
            at = 2 + 2 * (4 * chunk + sub)
            copies.append(pltpu.make_async_copy(normed_own.at[source], lhs.at[rows, pl.ds(0, tokens)], sems.at[at]))
            copies.append(
                pltpu.make_async_copy(normed_other.at[source], lhs.at[rows, pl.ds(tokens, tokens)], sems.at[at + 1])
            )
    tiles = slide_of.shape[1]
    half = w_proj.shape[0] // 2
    width = w_proj.shape[1]
    head = width // HEADS

    slide = slide_of[...].astype(F4)
    order = order_of[...].astype(F4)
    weight = jnp.zeros((tiles, tiles), F4)
    for branch in range(3):
        length = seg_len[branch].astype(F4)
        block = jnp.floor((order + 0.5) / length)
        dilation = float(2**branch)
        phase = order - dilation * jnp.floor(order * (1.0 / dilation))
        code = jnp.broadcast_to((slide * 64.0 + block) * 4.0 + phase, (tiles, tiles))
        weight = weight + (code == code.T).astype(F4)
    slide_col = jnp.broadcast_to(slide, (tiles, tiles)).T
    lane = lax.broadcasted_iota(jnp.int32, (tiles, 16), 1).astype(F4)
    member = (slide_col[:, :16] == lane).astype(F4).astype(BF)
    row = lax.broadcasted_iota(jnp.int32, (tiles, 2 * tiles), 0)
    col = lax.broadcasted_iota(jnp.int32, (tiles, 2 * tiles), 1)
    first = (row // 4) * 8 + row % 4
    loads[4].wait()
    every = gathered[...]
    left = dot_nn((col == first).astype(F4).astype(BF), every).astype(BF)
    right = dot_nn((col == first + 4).astype(F4).astype(BF), every).astype(BF)
    pooled_pair[:, :128] = left[:, half:]
    pooled_pair[:, 128:] = right[:, half:]
    loads[0].wait()
    rows = (dot_nn(left[:, :half], w_proj[:half, :]) + dot_nn(right[:, :half], w_proj[half:, :])).astype(BF)
    slide_rows[...] = rows
    loads[5].wait()
    cot_high, cot_low = halves(cot_all[...])
    d_attended = dot_nn(member, cot_high) + dot_nn(member, cot_low)
    loads[2].wait()
    d_context = dot_nt(d_attended.astype(BF), w_attn[...]).astype(BF)
    loads[1].wait()
    loads[3].start()
    for copy in copies:
        copy.start()
    qkv = dot_nn(rows, w_qkv[...]).astype(BF)

    scale = 1.0 / math.sqrt(head)
    group_heads = HEADS // 2
    group_width = group_heads * head
    lanes = lax.broadcasted_iota(jnp.int32, (1, group_width), 1)
    masks = [((lanes >= h * head) & (lanes < (h + 1) * head)).astype(F4).astype(BF) for h in range(group_heads)]

    def stacked(value):
        return jnp.concatenate([value * mask for mask in masks], axis=0)

    def beside(parts):
        return jnp.concatenate(parts, axis=1)

    grads = {}
    for group in range(2):
        start = group * group_width
        query = qkv[:, start : start + group_width]
        key_rows = qkv[:, width + start : width + start + group_width]
        value_rows = qkv[:, 2 * width + start : 2 * width + start + group_width]
        d_out = d_context[:, start : start + group_width]
        query_stack, d_out_stack = stacked(query), stacked(d_out)
        scores = dot_nt(query_stack, key_rows)
        d_share = dot_nt(d_out_stack, value_rows)
        shares, d_scores = [], []
        for h in range(group_heads):
            at = slice(h * tiles, (h + 1) * tiles)
            score = jnp.where(weight > 0.0, scores[at] * scale, -1e30)
            numerator = weight * jnp.exp(score - jnp.max(score, axis=1, keepdims=True))
            share = numerator * (1.0 / jnp.sum(numerator, axis=1, keepdims=True))
            slant = share * d_share[at]
            d_score = (slant - share * jnp.sum(slant, axis=1, keepdims=True)) * scale
            shares.append(share.astype(BF))
            d_scores.append(d_score.astype(BF))
        context[:, start : start + group_width] = dot_nn(beside(shares), stacked(value_rows))
        grads["query", group] = dot_nn(beside(d_scores), stacked(key_rows))
        grads["key", group] = dot_nn(beside([part.T for part in d_scores]), query_stack)
        grads["value", group] = dot_nn(beside([part.T for part in shares]), d_out_stack)
    d_qkv[...] = beside([grads[name, group].astype(BF) for name in ("query", "key", "value") for group in range(2)])
    d_direct[...] = d_attended

    near = pl.ds(pl.multiple_of(place[1] // 4 * 16, 16), 16)
    d_slide = d_direct[near, :] + dot_nt(d_qkv[near, :], w_qkv[...])
    d_embed = dot_nt(d_slide.astype(BF), w_proj[...])
    eight = jnp.where(place[1] // 2 % 2 == 0, d_embed[:8, :], d_embed[8:, :])
    high, low = halves(eight)
    loads[3].wait()
    back = dot_nt(jnp.concatenate([high, low], axis=0), w_out[...])
    back = back[:8, :] + back[8:, :]
    back = jnp.where(core == 0, back, jnp.concatenate([back[4:, :], back[:4, :]], axis=0)) * (4.0 / tokens)
    for copy in copies:
        copy.wait()
    patches = tokens // 4
    for tile in range(8):
        at = pl.ds(tile * patches, patches)
        d_preact[at, :] = (slope[at, :].astype(F4) * back[tile : tile + 1, :]).astype(BF)
    half_chunk = upper.shape[0]
    upper[...] = dot_nn(lhs2[:half_chunk, :], d_preact[...]).astype(BF)
    lower[...] = dot_nn(lhs2[half_chunk:, :], d_preact[...]).astype(BF)


def attention(place, seg_len, gathered, weights, cot_all, slide_of, order_of, normed, slopes):
    w_proj, w_qkv, w_attn, w_out = weights
    tiles = slide_of.shape[1]
    width, slide_width = w_proj.shape
    hidden = w_out.shape[0] // 2
    tokens = slopes[0].shape[0]
    return pl.pallas_call(
        attention_kernel,
        in_specs=[SMEM, SMEM] + [VMEM] * 2 + [ANY] * 10,
        out_specs=[VMEM] * 11,
        out_shape=[
            pltpu.VMEM((2 * tokens, hidden), BF),
            *[pltpu.VMEM((width // 4, 2 * tokens), BF)] * 3,
            *[jax.ShapeDtypeStruct((width // 8, hidden), BF)] * 2,
            jax.ShapeDtypeStruct((tiles, 3 * slide_width), BF),
            jax.ShapeDtypeStruct((tiles, slide_width), F4),
            jax.ShapeDtypeStruct((tiles, slide_width), F4),
            jax.ShapeDtypeStruct((tiles, slide_width), BF),
            jax.ShapeDtypeStruct((tiles, 256), BF),
        ],
        scratch_shapes=[
            pltpu.VMEM((width // 4, 2 * tokens), BF),
            pltpu.VMEM((2 * tokens, hidden), BF),
            pltpu.VMEM(w_proj.shape, BF),
            pltpu.VMEM(w_qkv.shape, BF),
            pltpu.VMEM(w_attn.shape, BF),
            pltpu.VMEM((hidden, width), BF),
            pltpu.VMEM(gathered.shape, BF),
            pltpu.VMEM(cot_all.shape, F4),
            pltpu.SemaphoreType.DMA((40,)),
        ],
        compiler_params=pltpu.CompilerParams(vmem_limit_bytes=28 * MIB),
        name="attention",
    )(
        place,
        seg_len,
        slide_of,
        order_of,
        *[from_hbm(value) for value in (gathered, cot_all, *weights, normed[0])],
        normed[1],
        from_hbm(slopes[0]),
        slopes[1],
    )


def embed_out_kernel(place, context, slide_rows, slide_of, counts, w_attn, slide_embed):
    tiles = slide_of.shape[1]
    group = lax.broadcasted_iota(jnp.int32, (16, tiles), 0)
    member = (slide_of[...] == group).astype(F4).astype(BF)
    high, low = halves(context[...])
    attended = slide_rows[...].astype(F4) + dot_nn(high, w_attn[...]) + dot_nn(low, w_attn[...])
    high, low = halves(attended)
    sums = (dot_nn(member, high) + dot_nn(member, low)) / counts[...].astype(F4)
    own = sums[0:4, :]
    for index in range(1, 4):
        own = jnp.where(place[0] == index, sums[4 * index : 4 * index + 4, :], own)
    slide_embed[...] = own


def embed_out(place, context, slide_rows, slide_of, counts, w_attn):
    return pl.pallas_call(
        embed_out_kernel,
        in_specs=[SMEM] + [VMEM] * 5,
        out_shape=jax.ShapeDtypeStruct((4, w_attn.shape[0]), F4),
        compiler_params=pltpu.CompilerParams(vmem_limit_bytes=12 * MIB),
        cost_estimate=pl.CostEstimate(flops=1000, bytes_accessed=1000, transcendentals=0),
        name="embed_out",
    )(place, context, slide_rows, slide_of, counts, w_attn)


def grad_out_kernel(pooled_pair, d_qkv, d_direct, w_qkv_hbm, w_proj_hbm, grad_out, w_qkv, w_proj, sems):
    pairs = [(w_qkv_hbm, w_qkv), (w_proj_hbm, w_proj)]
    loads = [pltpu.make_async_copy(src, dst, sems.at[i]) for i, (src, dst) in enumerate(pairs)]
    for load in loads:
        load.start()
    loads[0].wait()
    d_slide = d_direct[...] + dot_nt(d_qkv[...], w_qkv[...])
    loads[1].wait()
    high, low = halves(dot_nt(d_slide.astype(BF), w_proj[...]))
    pair = pooled_pair[...]
    both = dot_tn(pair, high) + dot_tn(pair, low)
    rows = grad_out.shape[0]
    grad_out[...] = both[:rows, :] + both[128 : 128 + rows, :]


def grad_out_of(pooled_pair, d_qkv, d_direct, weights, rows):
    return pl.pallas_call(
        grad_out_kernel,
        in_specs=[VMEM] * 3 + [ANY] * 2,
        out_shape=jax.ShapeDtypeStruct((rows, weights[1].shape[0]), F4),
        scratch_shapes=[pltpu.VMEM(weight.shape, BF) for weight in weights] + [pltpu.SemaphoreType.DMA((2,))],
        compiler_params=pltpu.CompilerParams(vmem_limit_bytes=20 * MIB),
        cost_estimate=pl.CostEstimate(flops=1000, bytes_accessed=1000, transcendentals=0),
        name="grad_out",
    )(pooled_pair, d_qkv, d_direct, *[from_hbm(weight) for weight in weights])


def grad_kernel(lhs, d_preact, *outs):
    rows = outs[0].shape[0]
    for index, out in enumerate(outs):
        out[...] = dot_nn(lhs[index * rows : (index + 1) * rows, :], d_preact[...]).astype(BF)


def grad_chunk(lhs, d_preact, parts=1):
    rows = lhs.shape[0]
    hidden = d_preact.shape[1]
    return pl.pallas_call(
        grad_kernel,
        in_specs=[VMEM] * 2,
        out_specs=[VMEM] * parts,
        out_shape=[jax.ShapeDtypeStruct((rows // parts, hidden), BF)] * parts,
        compiler_params=pltpu.CompilerParams(vmem_limit_bytes=16 * MIB),
        cost_estimate=pl.CostEstimate(flops=1000, bytes_accessed=1000, transcendentals=0),
        name="grad_chunk",
    )(from_vmem(lhs), from_vmem(d_preact))


def relay_kernel(up, down, up_received, down_received, after, up_out, down_out):
    half = up_received.shape[0]
    up_out[:half, :] = (up[:half, :].astype(F4) + up_received[...].astype(F4)).astype(BF)
    up_out[half:, :] = up[half:, :]
    down_out[:half, :] = down[:half, :]
    down_out[half:, :] = (down[half:, :].astype(F4) + down_received[...].astype(F4)).astype(BF)


def relay(up, down, up_received, down_received, after):
    return pl.pallas_call(
        relay_kernel,
        in_specs=[VMEM] * 4 + [ANY],
        out_shape=[jax.ShapeDtypeStruct(up.shape, BF)] * 2,
        compiler_params=pltpu.CompilerParams(vmem_limit_bytes=8 * MIB),
        name="relay",
    )(up, down, up_received, down_received, after)


def add_three_kernel(one, two, three, after, *outs):
    rows = outs[0].shape[0]
    for index, out in enumerate(outs):
        at = pl.ds(index * rows, rows)
        out[...] = (one[at, :].astype(F4) + two[at, :].astype(F4) + three[at, :].astype(F4)).astype(BF)


def add_three(parts, after):
    rows, columns = parts[0].shape
    return pl.pallas_call(
        add_three_kernel,
        in_specs=[VMEM] * 3 + [ANY],
        out_shape=[jax.ShapeDtypeStruct((rows // 4, columns), BF)] * 4,
        compiler_params=pltpu.CompilerParams(vmem_limit_bytes=8 * MIB),
        name="add_three",
    )(*parts, from_hbm(after))


def split_kernel(place, one, two, three, four, after, keep, send):
    total = (one[...].astype(F4) + two[...].astype(F4)) + (three[...].astype(F4) + four[...].astype(F4))
    rows = keep.shape[0]
    top, bottom = total[:rows, :], total[rows:, :]
    keep[...] = jnp.where(place[2] == 0, top, bottom)
    send[...] = jnp.where(place[2] == 0, bottom, top)


def split(place, parts, after):
    rows, columns = parts[0].shape
    return pl.pallas_call(
        split_kernel,
        in_specs=[SMEM] + [VMEM] * 4 + [ANY],
        out_shape=[jax.ShapeDtypeStruct((rows // 2, columns), F4)] * 2,
        compiler_params=pltpu.CompilerParams(vmem_limit_bytes=8 * MIB),
        name="split",
    )(place, *parts, from_hbm(after))


def finish_kernel(place, keep, received, out):
    half = out.shape[1] // 2
    first = place[2] == 0
    out[:, :half] = jnp.where(first, keep[...], received[...])
    out[:, half:] = jnp.where(first, received[...], keep[...])


def finish(place, keep, received):
    rows, columns = keep.shape
    return pl.pallas_call(
        finish_kernel,
        in_specs=[SMEM] + [VMEM] * 2,
        out_shape=jax.ShapeDtypeStruct((rows, 2 * columns), F4),
        compiler_params=pltpu.CompilerParams(vmem_limit_bytes=8 * MIB),
        name="finish",
    )(place, keep, received)


def moved(value, step):
    pairs = []
    for z in range(4):
        for x in range(4):
            for c in range(2):
                to_z, to_x, to_c = step(z, x, c)
                pairs.append(((z * 4 + x) * 2 + c, (to_z % 4 * 4 + to_x % 4) * 2 + to_c % 2))
    return lax.ppermute(value, "tile", pairs)


def other_core(value):
    return moved(value, lambda z, x, c: (z, x, c + 1))


def first_axis(value, k):
    return moved(value, lambda z, x, c: (z, x + k, c) if c == 0 else (z + k, x, c))


def second_axis(value, k):
    return moved(value, lambda z, x, c: (z + k, x, c) if c == 0 else (z, x + k, c))


def on_device(
    tiles,
    w_in,
    w_out,
    w_proj,
    w_qkv,
    w_attn_out,
    slide_of_tile,
    order_of_tile,
    slide_counts,
    seg_len,
    slide_cot,
):
    tile_count, patches, width = tiles.shape
    hidden = w_in.shape[1]
    peers = 32
    flat = tiles.reshape(tile_count * patches, width)
    tile_pos = lax.axis_index("tile")
    slide_pos = lax.axis_index("slide")
    place = jnp.stack([slide_pos, tile_pos, tile_pos % 2, tile_pos // 8, tile_pos // 2 % 4]).astype(jnp.int32)
    counts = slide_counts.reshape(-1, 1)
    slide_of = slide_of_tile.reshape(1, -1)
    order_of = order_of_tile.reshape(1, -1)

    slope_send, slope_keep, pooled, shared, token_mean, normed = forward(flat, w_in, w_out, slide_cot, tile_count)
    parts = [shared] + [
        lax.ppermute(shared, "slide", [(i, (i + k) % 4) for i in range(4)]) for k in (1, 2, 3)
    ]
    normed_t = transposed(normed, shared, 2 * patches)
    slices = pooled.reshape(2 * tile_count, peers, hidden // peers).transpose(1, 0, 2)
    slices = jnp.pad(slices.reshape(peers * 2 * tile_count, -1), ((0, 0), (0, 128 - hidden // peers)))
    mine, cot_all, normed_t, slope_send = embed(
        place, parts, token_mean, counts, slices, normed_t, slope_send, peers
    )
    gathered = lax.all_to_all(
        mine.reshape(peers, 8, -1), "tile", split_axis=0, concat_axis=0, tiled=True
    ).reshape(peers * 8, -1)
    slope_other, normed_other = other_core(slope_send), other_core(normed_t)
    d_preact, lhs0, lhs1, lhs3, upper, lower, d_qkv, d_direct, context, slide_rows, pooled_pair = attention(
        place,
        seg_len,
        gathered,
        (w_proj, w_qkv, w_attn_out, w_out),
        cot_all,
        slide_of,
        order_of,
        (normed_t, normed_other),
        (slope_keep, slope_other),
    )
    up_received, down_received = first_axis(upper, 1), first_axis(lower, 3)
    up, down = grad_chunk(lhs1, d_preact)[0], grad_chunk(lhs3, d_preact)[0]
    own = grad_chunk(lhs0, d_preact)[0]
    up, down = relay(up, down, up_received, down_received, own)
    parts = [own, first_axis(up, 1), first_axis(down, 3)]
    grad_out = grad_out_of(pooled_pair, d_qkv, d_direct, (w_qkv, w_proj), hidden // peers)
    slide_embed = embed_out(place, context, slide_rows, slide_of, counts, w_attn_out)
    parts = add_three(parts, grad_out)
    parts = [parts[0]] + [second_axis(parts[k], k) for k in (1, 2, 3)]
    keep, send = split(place, parts, slide_embed)
    return (slide_embed, finish(place, keep, other_core(send)), grad_out)


def solution(mesh):
    placed = (
        P("tile", None, None),
        P(None, "slide"),
        P("slide", None),
        P(),
        P(),
        P(),
        P(),
        P(),
        P(),
        P(),
        P("slide", None),
    )
    return jax.shard_map(
        on_device,
        mesh=mesh,
        in_specs=placed,
        out_specs=(P("slide", None), P("tile", "slide"), P(("slide", "tile"), None)),
        check_vma=False,
    )
```
